128 devices in a mesh: dp: 128 (over z, x, y, core).
Axes of the slice: x: 4, y: 4, z: 4, core: 2. Of those that a mesh axis runs over, the one named last changes fastest.
Arguments:
- queries: bfloat16 [65536, 1024], P('dp'), may hold values from -6 to 6
- resp_kv: bfloat16 [65536, 256], P('dp'), may hold values from -6 to 6
- prefix_kv: bfloat16 [8192, 256], P('dp'), may hold values from -6 to 6
- grad_out: bfloat16 [65536, 1024], P('dp'), may hold values from -6 to 6
- held_block: int32 [128], replicated, may hold values from 0 to 127, each once
- resp_prompt: int32 [128], replicated, may hold values from 0 to 3, as said below
- resp_len: int32 [128], replicated, may hold values from 64 to 512
Outputs:
- attn_out: bfloat16 [65536, 1024], P('dp')
- grad_q: bfloat16 [65536, 1024], P('dp')
- grad_resp_kv: bfloat16 [65536, 256], P('dp')
- grad_prefix_kv: float32 [8192, 256], P('dp')
The draws below stay inside these ranges and needn't reach their ends.
Inputs may be any that keep to these rules, and one draw needn't show every extreme that they name: `resp_prompt`: each prompt is named by exactly 32 devices.
All inputs are finite; a program needn't handle non-finite values.
Results may differ from the reference program's by a relative error of at most 0.0095.
Values may be sent and summed in bfloat16 or wider, within the bound.
A program may use at most 64 MiB of HBM per device.

```python
import jax
import jax.numpy as jnp
from jax import lax

HEAD_DIM = 128
HEADS = 8
PROMPT_LEN = 2048
PREFIX_DEV = 64
RESP_LEN = 512
PROMPTS = 4
GROUP = 32
N_DP = 128


def draw_queries(key, part):
    key = jax.random.fold_in(key, 5)
    first = jax.random.fold_in(key, 0)
    shape = (N_DP * RESP_LEN, HEADS * HEAD_DIM)
    values = jax.random.truncated_normal(first, -6.0, 6.0, shape, jnp.float32)
    return values.astype(jnp.bfloat16)


def draw_prefix_kv(key, part):
    key = jax.random.fold_in(key, 9)
    shape = (N_DP * PREFIX_DEV, 2 * HEAD_DIM)
    values = jax.random.truncated_normal(key, -6.0, 6.0, shape, jnp.float32)
    return values.astype(jnp.bfloat16)


def draw_resp_prompt(key, part):
    key = jax.random.fold_in(key, 11)
    order = jax.random.permutation(key, N_DP)
    return (order // GROUP).astype(jnp.int32)


def draw_resp_len(key, part):
    key = jax.random.fold_in(key, 23)
    first, second = jax.random.split(key)
    lengths = jax.random.randint(first, (N_DP,), RESP_LEN // 8, RESP_LEN + 1)
    longest = jax.random.randint(second, (), 0, N_DP)
    return lengths.at[longest].set(RESP_LEN).astype(jnp.int32)


def levels(key, extent, cuts, low, high):
    level = 1.0
    for axis_at, shards_of in cuts:
        steps = jax.random.uniform(jax.random.fold_in(jax.random.fold_in(key, 6), axis_at), (shards_of,), jnp.float32, low / len(cuts), high / len(cuts))
        level = level * jnp.repeat(jnp.exp(steps), extent[axis_at] // shards_of).reshape((-1,) + (1,) * (len(extent) - 1 - axis_at))
    return level


def noise(key, shape, spread, bound, cuts=(), kind=jnp.bfloat16):
    drawn = spread * jax.random.normal(key, shape, jnp.float32)
    if cuts:
        drawn = drawn * levels(key, shape, cuts, -0.22, 0.18)
    return jnp.clip(drawn, -bound, bound).astype(kind)


def setup_inputs(seed: int = 0) -> dict:
    streams_of = jax.random.split(jax.random.key(seed), 8)
    return {
        "queries": draw_queries(jax.random.fold_in(streams_of[7], 71), 0),
        "resp_kv": noise(streams_of[1], (N_DP * RESP_LEN, 2 * HEAD_DIM), 1.0, 6.0, ((0, 128),)),
        "prefix_kv": draw_prefix_kv(jax.random.fold_in(streams_of[7], 71), 0),
        "grad_out": noise(streams_of[3], (N_DP * RESP_LEN, HEADS * HEAD_DIM), 1.0, 6.0, ((0, 128),)),
        "held_block": jax.random.permutation(streams_of[4], N_DP).astype(jnp.int32),
        "resp_prompt": draw_resp_prompt(jax.random.fold_in(streams_of[7], 71), 0),
        "resp_len": draw_resp_len(jax.random.fold_in(streams_of[7], 71), 0),
    }


def attend(queries, key_rows, value_rows, grad_out, length, score_scale):
    row_count = queries.shape[0]
    head_width = key_rows.shape[1]
    head_count = queries.shape[1] // head_width
    key_count = key_rows.shape[0]
    prompt_rows = key_count - row_count
    head_group = max(1, min(head_count, 512 // row_count))
    while head_count % head_group != 0:
        head_group = head_group - 1
    block_count = head_count // head_group
    stacked = head_group * row_count
    live_rows = jnp.arange(row_count) < length
    masked = jnp.where(live_rows[:, None], grad_out, jnp.zeros((), grad_out.dtype))
    query_stack = queries.reshape(row_count, block_count, head_group, head_width).transpose(1, 2, 0, 3).reshape(block_count, stacked, head_width)
    grad_stack = masked.reshape(row_count, block_count, head_group, head_width).transpose(1, 2, 0, 3).reshape(block_count, stacked, head_width)
    position = jnp.tile(jnp.arange(row_count), head_group)
    column = jnp.arange(key_count)
    allowed = (column[None, :] < prompt_rows) | (column[None, :] - prompt_rows <= position[:, None])
    valid_rows = jnp.tile(live_rows, head_group)[:, None]

    def one_block(totals, inputs):
        key_grad, value_grad = totals
        query_block, grad_block = inputs
        scores = jnp.dot(query_block, key_rows.T, preferred_element_type=jnp.float32) * score_scale
        scores = jnp.where(allowed, scores, jnp.float32(-1e30))
        row_max = jnp.max(scores, axis=1, keepdims=True)
        exponent = jnp.exp(scores - row_max)
        weights = exponent / jnp.sum(exponent, axis=1, keepdims=True)
        weight_short = weights.astype(jnp.bfloat16)
        output = jnp.where(valid_rows, jnp.dot(weight_short, value_rows, preferred_element_type=jnp.float32), jnp.float32(0.0))
        weight_grad = jnp.dot(grad_block, value_rows.T, preferred_element_type=jnp.float32)
        row_delta = jnp.sum(grad_block.astype(jnp.float32) * output, axis=1, keepdims=True)
        score_grad = weights * (weight_grad - row_delta)
        score_short = score_grad.astype(jnp.bfloat16)
        query_grad = jnp.dot(score_short, key_rows, preferred_element_type=jnp.float32) * score_scale
        key_grad = key_grad + jnp.dot(score_short.T, query_block, preferred_element_type=jnp.float32) * score_scale
        value_grad = value_grad + jnp.dot(weight_short.T, grad_block, preferred_element_type=jnp.float32)
        return (key_grad, value_grad), (output.astype(jnp.bfloat16), query_grad.astype(jnp.bfloat16))

    start = (jnp.zeros((key_count, head_width), jnp.float32), jnp.zeros((key_count, head_width), jnp.float32))
    (key_grad, value_grad), (output, query_grad) = lax.scan(one_block, start, (query_stack, grad_stack))
    output = output.reshape(block_count, head_group, row_count, head_width).transpose(2, 0, 1, 3).reshape(row_count, head_count * head_width)
    query_grad = query_grad.reshape(block_count, head_group, row_count, head_width).transpose(2, 0, 1, 3).reshape(row_count, head_count * head_width)
    resp_grad = jnp.concatenate([key_grad[prompt_rows:], value_grad[prompt_rows:]], axis=1).astype(jnp.bfloat16)
    pref_grad = jnp.concatenate([key_grad[:prompt_rows], value_grad[:prompt_rows]], axis=1)
    return output, query_grad, resp_grad, pref_grad


def reference(queries, resp_kv, prefix_kv, grad_out, held_block, resp_prompt, resp_len):
    blocks_per = PROMPT_LEN // PREFIX_DEV
    pair_width = 2 * HEAD_DIM
    score_scale = 1.0 / (HEAD_DIM ** 0.5)
    location = jnp.argsort(held_block).astype(jnp.int32)
    blocks = prefix_kv.reshape(N_DP, PREFIX_DEV, pair_width)
    query_all = queries.reshape(N_DP, RESP_LEN, HEADS * HEAD_DIM)
    resp_pairs = resp_kv.reshape(N_DP, RESP_LEN, pair_width)
    grad_all = grad_out.reshape(N_DP, RESP_LEN, HEADS * HEAD_DIM)

    def step(totals, items):
        query_rows, pair_rows, grad_rows, prompt, length = items
        wanted = location[prompt * blocks_per + jnp.arange(blocks_per, dtype=jnp.int32)]
        prefix = blocks[wanted].reshape(PROMPT_LEN, pair_width)
        joined = jnp.concatenate([prefix, pair_rows], axis=0)
        output, query_grad, resp_grad, pref_grad = attend(query_rows, joined[:, :HEAD_DIM], joined[:, HEAD_DIM:], grad_rows, length, score_scale)
        totals = totals.at[prompt].add(pref_grad)
        return totals, (output, query_grad, resp_grad)

    start = jnp.zeros((PROMPTS, PROMPT_LEN, pair_width), jnp.float32)
    totals, (output, query_grad, resp_grad) = lax.scan(step, start, (query_all, resp_pairs, grad_all, resp_prompt, resp_len))
    per_block = totals.reshape(PROMPTS * blocks_per, PREFIX_DEV, pair_width)[held_block].reshape(N_DP * PREFIX_DEV, pair_width)
    return (output.reshape(N_DP * RESP_LEN, HEADS * HEAD_DIM), query_grad.reshape(N_DP * RESP_LEN, HEADS * HEAD_DIM),
            resp_grad.reshape(N_DP * RESP_LEN, pair_width), per_block)
```

```python
import functools
import math

import jax
import jax.numpy as jnp
from jax import lax
from jax.experimental import pallas as pl
from jax.experimental.pallas import tpu as pltpu
from jax.sharding import PartitionSpec as P

f32, bf16 = jnp.float32, jnp.bfloat16
NN = (((1,), (0,)), ((), ()))
NT = (((1,), (1,)), ((), ()))


def mm(a, b, dims=NN):
    return lax.dot_general(a, b, dims, preferred_element_type=f32)


def attend(length, q_ref, g_ref, rkv_ref, pkv_ref, o_ref, dq_ref, drkv_ref, dpkv_ref,
                kk, vv, kt, vt, s_scr, e_scr, dk, dv):
    rows, width = q_ref.shape
    d = 128
    heads = width // d
    np_ = pkv_ref.shape[0]
    nk = np_ + rows
    scale = 1.0 / math.sqrt(d)
    c = scale * math.log2(math.e)
    kk[0:np_, 0:d] = pkv_ref[:, 0:d]
    kk[0:np_, d:] = pkv_ref[:, 0:d]
    kk[np_:, 0:d] = rkv_ref[:, 0:d]
    kk[np_:, d:] = rkv_ref[:, 0:d]
    vv[0:np_, 0:d] = pkv_ref[:, d:]
    vv[np_:, 0:d] = rkv_ref[:, d:]
    vv[:, d:] = jnp.ones((nk, d), bf16)
    for i in range(0, nk, 512):
        kt[:, i:i + 512] = kk[i:i + 512, 0:d].T
        vt[:, i:i + 512] = vv[i:i + 512, 0:d].T
    dk[...] = jnp.zeros_like(dk)
    dv[...] = jnp.zeros_like(dv)
    live = lax.broadcasted_iota(jnp.int32, (1, rows), 1) < length
    half = rows // 2
    chunks = [(i, 512, 0) for i in range(0, np_, 512)] + [(np_, half, 0), (np_ + half, half, half)]
    tri = (lax.broadcasted_iota(jnp.int32, (half, half), 0)
           <= lax.broadcasted_iota(jnp.int32, (half, half), 1))

    def head(h, _):
        hs = pl.ds(pl.multiple_of(h * d, d), d)
        q = q_ref[:, hs]
        qs = q.astype(f32) * c
        qhi = qs.astype(bf16)
        qlo = (qs - qhi.astype(f32)).astype(bf16)
        q2t = jnp.concatenate([qhi, qlo], axis=1).T
        m = jnp.full((1, rows), -jnp.inf, f32)
        for k0, kn, r0 in chunks:
            s = mm(kk[k0:k0 + kn, :], q2t[:, r0:])
            if k0 >= np_:
                diag = jnp.where(tri, s[:, 0:half], -1e30)
                s = diag if r0 else jnp.concatenate([diag, s[:, half:]], axis=1)
            s_scr[k0:k0 + kn, r0:] = s
            cm = jnp.max(s, axis=0, keepdims=True)
            if r0:
                cm = jnp.concatenate([m[:, :r0], jnp.maximum(m[:, r0:], cm)], axis=1)
                m = cm
            else:
                m = jnp.maximum(m, cm)
        l = jnp.zeros((1, rows), f32)
        ot = jnp.zeros((d, rows), f32)
        for k0, kn, r0 in chunks:
            e = jnp.exp2(s_scr[k0:k0 + kn, r0:] - m[:, r0:])
            cl = jnp.sum(e, axis=0, keepdims=True)
            eb = e.astype(bf16)
            e_scr[k0:k0 + kn, r0:] = eb
            co = mm(vt[:, k0:k0 + kn], eb)
            if r0:
                l = jnp.concatenate([l[:, :r0], l[:, r0:] + cl], axis=1)
                ot = jnp.concatenate([ot[:, :r0], ot[:, r0:] + co], axis=1)
            else:
                l = l + cl
                ot = ot + co
        f = jnp.where(live, 1.0 / l, 0.0)
        ot = ot * f
        o_ref[:, hs] = ot.astype(bf16).T
        gt = g_ref[:, hs].T.astype(f32)
        gt = jnp.where(live, gt, 0.0)
        gpt = gt * f
        ndelta = -jnp.sum(gpt * ot, axis=0, keepdims=True)
        gptb = gpt.astype(bf16)
        gp = gptb.T
        dhi = ndelta.astype(bf16)
        dlo = (ndelta - dhi.astype(f32)).astype(bf16)
        sub = lax.broadcasted_iota(jnp.int32, (16, rows), 0)
        extra = jnp.where(sub == 0, dhi.astype(f32), jnp.where(sub == 1, dlo.astype(f32), 0.0)).astype(bf16)
        g2t = jnp.concatenate([gptb, extra, jnp.zeros((d - 16, rows), bf16)], axis=0)
        dqt = jnp.zeros((d, rows), f32)
        for k0, kn, r0 in chunks:
            dp = mm(vv[k0:k0 + kn, :], g2t[:, r0:])
            eb = e_scr[k0:k0 + kn, r0:]
            ds = eb * dp.astype(bf16)
            cq = mm(kt[:, k0:k0 + kn], ds)
            if r0:
                dqt = jnp.concatenate([dqt[:, :r0], dqt[:, r0:] + cq], axis=1)
            else:
                dqt = dqt + cq
            dk[k0:k0 + kn, :] += mm(ds, q[r0:, :])
            dv[k0:k0 + kn, :] += mm(eb, gp[r0:, :])
        dq_ref[:, hs] = (dqt * scale).astype(bf16).T
        return 0

    lax.fori_loop(0, heads, head, 0)
    nb = np_ // 64
    drkv_ref[:, 0:d] = (dk[np_:, :] * scale).astype(bf16)
    drkv_ref[:, d:] = dv[np_:, :].astype(bf16)
    dpkv_ref[:, 0:64, :] = (dk[0:np_, :] * scale).astype(bf16).reshape(nb, 64, d)
    dpkv_ref[:, 64:, :] = dv[0:np_, :].astype(bf16).reshape(nb, 64, d)


MESH = pl.DeviceIdType.MESH
SIDE = 4


def place():
    me = lax.axis_index("dp")
    return (me // 32, me // 8 % 4, me // 2 % 4), me % 2


def device(at, core):
    return ((at[0] * SIDE + at[1]) * SIDE + at[2]) * 2 + core


def moved(at, axis, step):
    return tuple((c + step + SIDE) % SIDE if a == axis else c for a, c in enumerate(at))


def enter(at, core):
    barrier = pltpu.get_barrier_semaphore()
    near = [device(moved(at, a, s), core) for a in range(3) for s in (1, -1)] + [device(at, 1 - core)]
    for n in near:
        pl.semaphore_signal(barrier, inc=1, device_id=(n,), device_id_type=MESH)
    pl.semaphore_wait(barrier, len(near))


class Sender:
    def __init__(self, send, recv):
        self.send, self.recv, self.count, self.all = send, recv, 0, []

    def __call__(self, src, dst, to):
        i = self.count
        self.count += 1
        c = pltpu.make_async_remote_copy(src_ref=src, dst_ref=dst, send_sem=self.send.at[i], recv_sem=self.recv.at[i],
                                         device_id=(to,), device_id_type=MESH)
        c.start()
        self.all.append(c)
        return c

    def drain(self):
        for c in self.all:
            c.wait_send()


AG_PARTS = [((0, 48), (0, 128), (0, 1, 2)), ((0, 48), (128, 256), (1, 2, 0)), ((48, 64), (0, 256), (2, 0, 1))]


def gather(go, loc_ref, prompt, x_ref, out_ref, g):
    at, core = place()
    sib = device(at, 1 - core)
    g[at[0], at[1], at[2], core] = x_ref[...]

    def view(part, idx):
        (r0, r1), (c0, c1), _ = part
        return g.at[idx[0], idx[1], idx[2], core, r0:r1, c0:c1]

    def block(order, i, k, half=None):
        idx = []
        for a in range(3):
            if a in order[:i]:
                if half is not None and a == order[0]:
                    idx.append(slice(2 * half, 2 * half + 2))
                else:
                    idx.append(slice(0, SIDE))
            elif a == order[i]:
                idx.append(k)
            else:
                idx.append(at[a])
        return idx

    def half_view(part, i, k, half):
        (r0, r1), (c0, c1), order = part
        if i > 0:
            return view(part, block(order, i, k, half))
        idx = block(order, i, k)
        if r1 - r0 >= 32:
            rr = (r0, r0 + 32) if half == 0 else (r0 + 32, r1)
            return g.at[idx[0], idx[1], idx[2], core, rr[0]:rr[1], c0:c1]
        cc = (c0, c0 + 128) if half == 0 else (c0 + 128, c1)
        return g.at[idx[0], idx[1], idx[2], core, r0:r1, cc[0]:cc[1]]

    def to_sib(part, idx):
        v = view(part, idx)
        return go(v, v, sib)

    late = []
    for i in range(3):
        first = []
        for part in AG_PARTS:
            order = part[2]
            a = order[i]
            p = at[a]
            v = view(part, block(order, i, p))
            up = go(v, v, device(moved(at, a, 1), core))
            down = go(v, v, device(moved(at, a, -1), core))
            first.append((up, down))
        if i == 2:
            for part in AG_PARTS:
                late.append(to_sib(part, block(part[2], 2, at[part[2][2]])))
        second = []
        for part, (up, down) in zip(AG_PARTS, first):
            order = part[2]
            a = order[i]
            below, above = (at[a] + 3) % SIDE, (at[a] + 1) % SIDE
            up.wait_recv()
            v = half_view(part, i, below, 0)
            u2 = go(v, v, device(moved(at, a, 1), core))
            if i == 2:
                late.append(to_sib(part, block(order, 2, below)))
            down.wait_recv()
            v = half_view(part, i, above, 1)
            d2 = go(v, v, device(moved(at, a, -1), core))
            if i == 2:
                late.append(to_sib(part, block(order, 2, above)))
            second.append((u2, d2))
        for part, (u2, d2) in zip(AG_PARTS, second):
            order = part[2]
            u2.wait_recv()
            d2.wait_recv()
            if i == 2:
                late.append(to_sib(part, block(order, 2, (at[order[2]] + 2) % SIDE)))
    for c in late:
        c.wait_recv()
    for b in range(32):
        n = loc_ref[prompt * 32 + b]
        out_ref[b * 64:(b + 1) * 64, :] = g[n // 32, n // 8 % 4, n // 2 % 4, n % 2]


RS_PARTS = [((0, 48), (0, 1, 2)), ((48, 96), (1, 2, 0)), ((96, 128), (2, 0, 1))]


def scatter(go, held_ref, prompt_ref, x_ref, out_ref, w, peer, bufs):
    at, core = place()
    sib = device(at, 1 - core)
    swap = go(x_ref, peer, sib)
    mine, other = prompt_ref[device(at, core)], prompt_ref[sib]
    zero = jnp.zeros((128, 128), bf16)

    def fill(j, _):
        b = held_ref[j * 2 + core]
        w[j // 16, j // 4 % 4, j % 4] = jnp.where(b // 32 == mine, x_ref[b % 32], zero)
        return 0

    def more(j, _):
        b = held_ref[j * 2 + core]
        w[j // 16, j // 4 % 4, j % 4] += jnp.where(b // 32 == other, peer[b % 32], zero)
        return 0

    lax.fori_loop(0, 64, fill, 0)
    swap.wait_recv()
    lax.fori_loop(0, 64, more, 0)

    def spot(part, i, k, half=None):
        (r0, r1), order = part
        idx, free = [], None
        for a in range(3):
            if a in order[:i]:
                idx.append(at[a])
            elif a == order[i]:
                idx.append(k)
            else:
                free = a if free is None else free
                idx.append(slice(2 * half, 2 * half + 2) if half is not None and free == a else slice(0, SIDE))
        if half is not None and free is None:
            mid = r0 + (32 if r1 - r0 == 48 else 16)
            r0, r1 = (r0, mid) if half == 0 else (mid, r1)
        return (*idx, slice(r0, r1), slice(None))

    def inner(part, i, half):
        (r0, r1), _ = part
        if i < 2:
            return (slice(2 * half, 2 * half + 2),)
        mid = 32 if r1 - r0 == 48 else 16
        return (slice(0, mid) if half == 0 else slice(mid, r1 - r0),)

    for i in range(3):
        first = []
        for n, part in enumerate(RS_PARTS):
            a = part[1][i]
            p = at[a]
            up, down = device(moved(at, a, 1), core), device(moved(at, a, -1), core)
            far, above, below = (p + 2) % SIDE, (p + 1) % SIDE, (p + 3) % SIDE
            near_buf, far_buf = bufs[2 * (3 * n + i)], bufs[2 * (3 * n + i) + 1]
            f0 = go(w.at[spot(part, i, far, 0)], far_buf.at[(0, *inner(part, i, 0))], up)
            f1 = go(w.at[spot(part, i, far, 1)], far_buf.at[(1, *inner(part, i, 1))], down)
            n0 = go(w.at[spot(part, i, above, 1)], near_buf.at[(0, *inner(part, i, 1))], up)
            n1 = go(w.at[spot(part, i, below, 0)], near_buf.at[(1, *inner(part, i, 0))], down)
            first.append((f0, f1, n0, n1))
        second = []
        for n, (part, (f0, f1, n0, n1)) in enumerate(zip(RS_PARTS, first)):
            a = part[1][i]
            p = at[a]
            up, down = device(moved(at, a, 1), core), device(moved(at, a, -1), core)
            above, below = (p + 1) % SIDE, (p + 3) % SIDE
            near_buf, far_buf = bufs[2 * (3 * n + i)], bufs[2 * (3 * n + i) + 1]
            f0.wait_recv()
            w[spot(part, i, above, 0)] += far_buf[(0, *inner(part, i, 0))]
            s0 = go(w.at[spot(part, i, above, 0)], near_buf.at[(0, *inner(part, i, 0))], up)
            f1.wait_recv()
            w[spot(part, i, below, 1)] += far_buf[(1, *inner(part, i, 1))]
            s1 = go(w.at[spot(part, i, below, 1)], near_buf.at[(1, *inner(part, i, 1))], down)
            second.append((s0, s1))
        for n, (part, (f0, f1, n0, n1), (s0, s1)) in enumerate(zip(RS_PARTS, first, second)):
            for c in (n0, n1, s0, s1):
                c.wait_recv()
            near_buf = bufs[2 * (3 * n + i)]
            p = at[part[1][i]]
            total = (w[spot(part, i, p)].astype(f32) + near_buf[0].astype(f32)) + near_buf[1].astype(f32)
            if i < 2:
                w[spot(part, i, p)] = total.astype(bf16)
            else:
                (r0, r1), _ = part
                for s0, s1, col in ((r0, min(r1, 64), 0), (max(r0, 64), r1, 128)):
                    if s1 > s0:
                        out_ref[s0 % 64:s0 % 64 + s1 - s0, col:col + 128] = total[s0 - r0:s1 - r0]


def kernel(loc_ref, held_ref, prompt_ref, len_ref, q_ref, g_ref, rkv_ref, x_ref, o_ref, dq_ref, drkv_ref, out_ref,
           blocks, pkv, dpkv, kk, vv, kt, vt, s_scr, e_scr, dk, dv, w, peer, *rest):
    bufs, (send, recv) = rest[:-2], rest[-2:]
    at, core = place()
    me = device(at, core)
    enter(at, core)
    go = Sender(send, recv)
    gather(go, loc_ref, prompt_ref[me], x_ref, pkv, blocks)
    attend(len_ref[me], q_ref, g_ref, rkv_ref, pkv, o_ref, dq_ref, drkv_ref, dpkv, kk, vv, kt, vt, s_scr, e_scr, dk, dv)
    scatter(go, held_ref, prompt_ref, dpkv, out_ref, w, peer, bufs)
    go.drain()


def on_device(queries, resp_kv, prefix_kv, grad_out, held_block, resp_prompt, resp_len):
    spots = jnp.arange(128, dtype=jnp.int32)
    loc = jnp.sum(jnp.where(held_block[None, :] == spots[:, None], spots[None, :], 0), axis=1).astype(jnp.int32)
    rows, nk = queries.shape[0], 2048 + queries.shape[0]
    bufs = []
    for (r0, r1), order in RS_PARTS:
        for i in range(3):
            shape = (SIDE,) * (2 - i) + (r1 - r0, 128)
            bufs += [pltpu.VMEM((2,) + shape, bf16)] * 2
    sm = pl.BlockSpec(memory_space=pltpu.SMEM)
    vm = pl.BlockSpec(memory_space=pltpu.VMEM)
    return pl.pallas_call(
        kernel,
        out_shape=(jax.ShapeDtypeStruct(queries.shape, bf16), jax.ShapeDtypeStruct(queries.shape, bf16),
                   jax.ShapeDtypeStruct(resp_kv.shape, bf16), jax.ShapeDtypeStruct((64, 256), f32)),
        in_specs=[sm] * 4 + [vm] * 4,
        out_specs=(vm,) * 4,
        scratch_shapes=[pltpu.VMEM((4, 4, 4, 2, 64, 256), bf16), pltpu.VMEM((2048, 256), bf16),
                        pltpu.VMEM((32, 128, 128), bf16),
                        pltpu.VMEM((nk, 256), bf16), pltpu.VMEM((nk, 256), bf16), pltpu.VMEM((128, nk), bf16),
                        pltpu.VMEM((128, nk), bf16), pltpu.VMEM((nk, rows), f32), pltpu.VMEM((nk, rows), bf16),
                        pltpu.VMEM((nk, 128), f32), pltpu.VMEM((nk, 128), f32),
                        pltpu.VMEM((4, 4, 4, 128, 128), bf16), pltpu.VMEM((32, 128, 128), bf16)] + bufs
        + [pltpu.SemaphoreType.DMA((103,)), pltpu.SemaphoreType.DMA((103,))],
        compiler_params=pltpu.CompilerParams(collective_id=0, has_side_effects=True, vmem_limit_bytes=60 * 2**20),
        name="shared",
    )(loc, held_block, resp_prompt, resp_len, queries, grad_out, resp_kv, prefix_kv)


def solution(mesh):
    rows = P("dp", None)
    return jax.shard_map(on_device, mesh=mesh, in_specs=(rows, rows, rows, rows, P(), P(), P()),
                         out_specs=(rows, rows, rows, rows), check_vma=False)
```

```python
import math

import jax
import jax.numpy as jnp
from jax import lax
from jax.experimental import pallas as pl
from jax.experimental.pallas import tpu as pltpu
from jax.sharding import PartitionSpec as P

f32, bf16 = jnp.float32, jnp.bfloat16
MESH = pl.DeviceIdType.MESH
NN = (((1,), (0,)), ((), ()))
SIDE = 4
D = 128
HEADS = 8
ROWS = 512
BLOCKS = 32
CHUNKS = 4
CK = 512
PK = CHUNKS * CK
NK = PK + ROWS
HALF = ROWS // 2
UNROLL = 4
SCALE = 1.0 / math.sqrt(D)
LOG2 = SCALE * math.log2(math.e)
ORDERS = ((0, 1, 2), (1, 2, 0), (2, 0, 1))
HOPS = (2, 1, 3)
PARTS = [(c, t) for c in range(CHUNKS) for t in range(2)]


def mm(a, b):
    return lax.dot_general(a, b, NN, preferred_element_type=f32)


def place():
    me = lax.axis_index("dp")
    return (me // 32, me // 8 % SIDE, me // 2 % SIDE), me % 2


def device(at, core):
    return ((at[0] * SIDE + at[1]) * SIDE + at[2]) * 2 + core


def moved(at, axis, step):
    return tuple((c + step) % SIDE if a == axis else c for a, c in enumerate(at))


class Sender:
    def __init__(self, send, recv):
        self.send, self.recv, self.count, self.all = send, recv, 0, []

    def __call__(self, src, dst, to):
        i = self.count
        self.count += 1
        c = pltpu.make_async_remote_copy(src_ref=src, dst_ref=dst, send_sem=self.send.at[i], recv_sem=self.recv.at[i],
                                         device_id=(to,), device_id_type=MESH)
        c.start()
        self.all.append(c)
        return c

    def drain(self):
        for c in self.all:
            c.wait_send()


class Gather:
    def __init__(self, go, at, core, refs):
        self.go, self.at, self.core, self.refs = go, at, core, refs
        self.flying = {}

    def order(self, n):
        return ORDERS[(n + 1) % 3]

    def view(self, n, i, k):
        order = self.order(n)
        idx = [slice(0, SIDE) if a in order[:i] else k if a == order[i] else self.at[a] for a in range(3)]
        return self.refs[n].at[(self.core, *idx)]

    def start(self, n, i):
        a = self.order(n)[i]
        v = self.view(n, i, self.at[a])
        self.flying[n, i] = [self.go(v, v, device(moved(self.at, a, s), self.core)) for s in HOPS]

    def wait(self, n, i):
        for c in self.flying[n, i]:
            c.wait_recv()

    def start_core(self, n):
        v = self.refs[n].at[self.core]
        self.flying[n, 3] = [self.go(v, v, device(self.at, 1 - self.core))]


class Scatter:
    def __init__(self, go, at, core, held, prompt, own, peer, w, bufs, out):
        self.go, self.at, self.core, self.held, self.prompt = go, at, core, held, prompt
        self.own, self.peer, self.w, self.bufs, self.out = own, peer, w, bufs, out
        self.flying = {}

    def swap(self, c):
        self.flying[c] = self.go(self.own[c], self.peer[c], device(self.at, 1 - self.core))

    def fill(self, c):
        self.flying[c].wait_recv()
        mine = self.prompt[device(self.at, self.core)]
        other = self.prompt[device(self.at, 1 - self.core)]
        own, peer, w = self.own[c], self.peer[c], self.w[c]
        zero = jnp.zeros((32, D), bf16)

        def body(j, _):
            for u in range(4):
                b = self.held[(j * 4 + u) * 2 + self.core]
                p, k = lax.shift_right_logical(b, 5), lax.bitwise_and(b, 31)
                w[j // 4, j % 4, u] = jnp.where(p == mine, own[k], zero) + jnp.where(p == other, peer[k], zero)
            return 0

        lax.fori_loop(0, 16, body, 0)

    def spot(self, n, i, k):
        c, t = PARTS[n]
        order = ORDERS[n % 3]
        idx = [self.at[a] if a in order[:i] else k if a == order[i] else slice(0, SIDE) for a in range(3)]
        return (*idx, slice(16 * t, 16 * t + 16), slice(None))

    def start(self, c, i):
        for n in (2 * c, 2 * c + 1):
            a = ORDERS[n % 3][i]
            self.flying[n, i] = [
                self.go(self.w[c].at[self.spot(n, i, (self.at[a] + s) % SIDE)], self.bufs[3 * n + i].at[j],
                        device(moved(self.at, a, s), self.core)) for j, s in enumerate(HOPS)]

    def add(self, c, i):
        for n in (2 * c, 2 * c + 1):
            for f in self.flying[n, i]:
                f.wait_recv()
            buf = self.bufs[3 * n + i]
            here = self.spot(n, i, self.at[ORDERS[n % 3][i]])
            total = (self.w[c][here].astype(f32) + buf[0].astype(f32)) + (buf[1].astype(f32) + buf[2].astype(f32))
            if i < 2:
                self.w[c][here] = total.astype(bf16)
            else:
                t = n % 2
                self.out[16 * c:16 * c + 16, D * t:D * t + D] = total

    def stage(self, c, s):
        if s == 0:
            self.fill(c)
            self.start(c, 0)
        else:
            self.add(c, s - 1)
            if s < 3:
                self.start(c, s)


def kernel(loc_ref, held_ref, prompt_ref, len_ref, q_hbm, g_hbm, rkv_ref, x_ref, o_ref, dq_ref, drkv_ref, out_ref, *rest):
    gref, rest = rest[:8], rest[8:]
    own, peer, w, bufs, rest = rest[:4], rest[4:8], rest[8:12], rest[12:36], rest[36:]
    q_ref, g_ref, kk, vv, kt, vt, q2t, g2t, gp, e_all, ms, ls, ot, dqt, dk, dv, s0, s1, p0, p1, send, recv, local = rest
    at, core = place()
    me = device(at, core)
    barrier = pltpu.get_barrier_semaphore()
    near = [device(moved(at, a, s), core) for a in range(3) for s in HOPS] + [device(at, 1 - core)]
    for n in near:
        pl.semaphore_signal(barrier, inc=1, device_id=(n,), device_id_type=MESH)
    q_in = pltpu.make_async_copy(q_hbm, q_ref, local.at[0])
    g_in = pltpu.make_async_copy(g_hbm, g_ref, local.at[1])
    q_in.start()
    g_in.start()
    go = Sender(send, recv)
    gather = Gather(go, at, core, gref)
    for n, (c, t) in enumerate(PARTS):
        gref[n][core, at[0], at[1], at[2]] = x_ref[16 * c:16 * c + 16, D * t:D * t + D]
    pl.semaphore_wait(barrier, len(near))
    for n in range(8):
        gather.start(n, 0)

    length = len_ref[me]
    live = lax.broadcasted_iota(jnp.int32, (1, ROWS), 1) < length
    tri = lax.broadcasted_iota(jnp.int32, (HALF, HALF), 0) <= lax.broadcasted_iota(jnp.int32, (HALF, HALF), 1)
    vv[:, D:] = jnp.ones((NK, D), bf16)

    def heads_loop(lo, hi, item, step=UNROLL):
        def body(i, _):
            for u in range(step):
                item(i * step + u)
            return 0
        lax.fori_loop(lo // step, hi // step, body, 0)

    def staged(ahead, item, slots):
        slots[0][...] = ahead(0)

        def body(i, _):
            for u in range(UNROLL):
                h = i * UNROLL + u
                slots[(u + 1) % 2][...] = ahead(lax.rem(h + 1, HEADS))
                item(h, slots[u % 2])
            return 0
        lax.fori_loop(0, HEADS // UNROLL, body, 0)

    def cols(h):
        return pl.ds(pl.multiple_of(h * D, D), D)

    def prepare(h):
        qs = q_ref[:, cols(h)].astype(f32) * LOG2
        hi = qs.astype(bf16)
        lo = (qs - hi.astype(f32)).astype(bf16)
        q2t[h, 0:D] = hi.T
        q2t[h, D:] = lo.T

    def place_keys(k0, kn, keys, vals):
        kk[k0:k0 + kn, 0:D] = keys
        kk[k0:k0 + kn, D:] = keys
        vv[k0:k0 + kn, 0:D] = vals

    def turn(k0, kn):
        kt[:, k0:k0 + kn] = kk[k0:k0 + kn, 0:D].T
        vt[:, k0:k0 + kn] = vv[k0:k0 + kn, 0:D].T

    def first(h):
        sa = mm(kk[PK:PK + HALF, :], q2t[h])
        sa = jnp.concatenate([jnp.where(tri, sa[:, :HALF], -1e30), sa[:, HALF:]], axis=1)
        sb = jnp.where(tri, mm(kk[PK + HALF:, :], q2t[h, :, HALF:]), -1e30)
        m = jnp.max(sa, axis=0, keepdims=True)
        m = jnp.concatenate([m[:, :HALF], jnp.maximum(m[:, HALF:], jnp.max(sb, axis=0, keepdims=True))], axis=1)
        ea = jnp.exp2(sa - m)
        eb = jnp.exp2(sb - m[:, HALF:])
        l = jnp.sum(ea, axis=0, keepdims=True)
        l = jnp.concatenate([l[:, :HALF], l[:, HALF:] + jnp.sum(eb, axis=0, keepdims=True)], axis=1)
        ea, eb = ea.astype(bf16), eb.astype(bf16)
        e_all[h, PK:PK + HALF, :] = ea
        e_all[h, PK + HALF:, HALF:] = eb
        oa = mm(vt[:, PK:PK + HALF], ea)
        ob = mm(vt[:, PK + HALF:], eb)
        ms[0, h] = m
        ls[h] = l
        ot[h, :, 0:HALF] = oa[:, :HALF]
        ot[h, :, HALF:] = oa[:, HALF:] + ob

    def forward(c):
        k0 = c * CK

        def ahead(h):
            return mm(kk[k0:k0 + CK, :], q2t[h])

        def item(h, s):
            old = ms[c, h]
            m = jnp.maximum(old, jnp.max(s[...], axis=0, keepdims=True))
            e = jnp.exp2(s[...] - m)
            fade = jnp.exp2(old - m)
            ls[h] = ls[h] * fade + jnp.sum(e, axis=0, keepdims=True)
            e = e.astype(bf16)
            e_all[h, k0:k0 + CK, :] = e
            ot[h] = ot[h] * fade + mm(vt[:, k0:k0 + CK], e)
            ms[c + 1, h] = m
        staged(ahead, item, (s0, s1))

    def finish(h):
        f = jnp.where(live, 1.0 / ls[h], 0.0)
        o = ot[h] * f
        o_ref[:, cols(h)] = o.astype(bf16).T
        gt = g_ref[:, cols(h)].T.astype(f32)
        gt = jnp.where(live, gt, 0.0) * f
        neg = -jnp.sum(gt * o, axis=0, keepdims=True)
        gb = gt.astype(bf16)
        gp[h] = gb.T
        hi = neg.astype(bf16).astype(f32)
        sub = lax.broadcasted_iota(jnp.int32, (16, ROWS), 0)
        extra = jnp.where(sub == 0, hi, jnp.where(sub == 1, neg - hi, 0.0)).astype(bf16)
        g2t[h, 0:D] = gb
        g2t[h, D:D + 16] = extra
        g2t[h, D + 16:] = jnp.zeros((D - 16, ROWS), bf16)
        dqt[h] = jnp.zeros((D, ROWS), f32)

    def slope(h, k0, kn, r0):
        return mm(vv[k0:k0 + kn, :], g2t[h, :, r0:]).astype(bf16)

    def back(h, dp, k0, kn, r0, stage, a0):
        fade = jnp.exp2(ms[stage, h] - ms[CHUNKS, h]).astype(bf16)[:, r0:]
        e = e_all[h, k0:k0 + kn, r0:] * fade
        ds = e * dp
        dqt[h, :, r0:] += mm(kt[:, k0:k0 + kn], ds)
        dk[a0:a0 + kn, :] += mm(ds, q_ref[r0:, cols(h)])
        dv[a0:a0 + kn, :] += mm(e, gp[h, r0:, :])

    def load_chunk(c):
        for n in (2 * c, 2 * c + 1):
            gather.wait(n, 3)
        prompt = prompt_ref[me]
        for b in range(BLOCKS):
            n = loc_ref[prompt * BLOCKS + b]
            idx = (lax.bitwise_and(n, 1), lax.shift_right_logical(n, 5), lax.bitwise_and(lax.shift_right_logical(n, 3), 3),
                   lax.bitwise_and(lax.shift_right_logical(n, 1), 3))
            place_keys(c * CK + 16 * b, 16, gref[2 * c][idx], gref[2 * c + 1][idx])
        turn(c * CK, CK)

    place_keys(PK, ROWS, rkv_ref[:, 0:D], rkv_ref[:, D:])
    turn(PK, ROWS)
    q_in.wait()
    heads_loop(0, HEADS, prepare)
    for n in range(8):
        gather.wait(n, 0)
        gather.start(n, 1)
    heads_loop(0, 4, first)
    for n in range(8):
        gather.wait(n, 1)
        gather.start(n, 2)
    heads_loop(4, HEADS, first)

    def pass_on(c):
        for n in (2 * c, 2 * c + 1):
            gather.wait(n, 2)
            gather.start_core(n)

    pass_on(0)
    for c in range(CHUNKS):
        load_chunk(c)
        if c + 1 < CHUNKS:
            pass_on(c + 1)
        forward(c)
    g_in.wait()
    heads_loop(0, HEADS, finish)

    scatter = Scatter(go, at, core, held_ref, prompt_ref, own, peer, w, bufs, out_ref)
    for c in range(CHUNKS):
        dk[...] = jnp.zeros_like(dk)
        dv[...] = jnp.zeros_like(dv)
        staged(lambda h: slope(h, c * CK, CK, 0), lambda h, dp: back(h, dp[...], c * CK, CK, 0, c + 1, 0), (p0, p1))
        own[c][:, 0:16, :] = (dk[...] * SCALE).astype(bf16).reshape(BLOCKS, 16, D)
        own[c][:, 16:, :] = dv[...].astype(bf16).reshape(BLOCKS, 16, D)
        scatter.swap(c)
        for s in range(c):
            scatter.stage(c - 1 - s, s)
    dk[...] = jnp.zeros_like(dk)
    dv[...] = jnp.zeros_like(dv)

    def last(h):
        back(h, slope(h, PK, HALF, 0), PK, HALF, 0, 0, 0)
        back(h, slope(h, PK + HALF, HALF, HALF), PK + HALF, HALF, HALF, 0, HALF)
        dq_ref[:, cols(h)] = (dqt[h] * SCALE).astype(bf16).T

    heads_loop(0, 4, last)
    for s in range(4):
        scatter.stage(3 - s, s)
    heads_loop(4, HEADS, last)
    for s in range(1, 4):
        scatter.stage(4 - s, s)
    drkv_ref[:, 0:D] = (dk[...] * SCALE).astype(bf16)
    drkv_ref[:, D:] = dv[...].astype(bf16)
    scatter.stage(3, 2)
    scatter.stage(2, 3)
    scatter.stage(3, 3)
    go.drain()


def on_device(queries, resp_kv, prefix_kv, grad_out, held_block, resp_prompt, resp_len):
    spots = jnp.arange(128, dtype=jnp.int32)
    loc = jnp.sum(jnp.where(held_block[None, :] == spots[:, None], spots[None, :], 0), axis=1).astype(jnp.int32)
    bufs = []
    for n in range(8):
        for i in range(3):
            bufs.append(pltpu.VMEM((3,) + (SIDE,) * (2 - i) + (16, D), bf16))
    sm = pl.BlockSpec(memory_space=pltpu.SMEM)
    vm = pl.BlockSpec(memory_space=pltpu.VMEM)
    hbm = pl.BlockSpec(memory_space=pl.ANY)
    sems = 8 * 10 + 8 * 9 + 4
    return pl.pallas_call(
        kernel,
        out_shape=(jax.ShapeDtypeStruct(queries.shape, bf16), jax.ShapeDtypeStruct(queries.shape, bf16),
                   jax.ShapeDtypeStruct(resp_kv.shape, bf16), jax.ShapeDtypeStruct((64, 256), f32)),
        in_specs=[sm] * 4 + [hbm] * 2 + [vm] * 2,
        out_specs=(vm,) * 4,
        scratch_shapes=[pltpu.VMEM((2, SIDE, SIDE, SIDE, 16, D), bf16)] * 8
        + [pltpu.VMEM((BLOCKS, 32, D), bf16)] * 8 + [pltpu.VMEM((SIDE, SIDE, SIDE, 32, D), bf16)] * 4 + bufs
        + [pltpu.VMEM((ROWS, HEADS * D), bf16), pltpu.VMEM((ROWS, HEADS * D), bf16),
           pltpu.VMEM((NK, 2 * D), bf16), pltpu.VMEM((NK, 2 * D), bf16), pltpu.VMEM((D, NK), bf16),
           pltpu.VMEM((D, NK), bf16), pltpu.VMEM((HEADS, 2 * D, ROWS), bf16), pltpu.VMEM((HEADS, 2 * D, ROWS), bf16),
           pltpu.VMEM((HEADS, ROWS, D), bf16), pltpu.VMEM((HEADS, NK, ROWS), bf16),
           pltpu.VMEM((CHUNKS + 1, HEADS, 1, ROWS), f32), pltpu.VMEM((HEADS, 1, ROWS), f32),
           pltpu.VMEM((HEADS, D, ROWS), f32), pltpu.VMEM((HEADS, D, ROWS), f32),
           pltpu.VMEM((ROWS, D), f32), pltpu.VMEM((ROWS, D), f32),
           pltpu.VMEM((CK, ROWS), f32), pltpu.VMEM((CK, ROWS), f32), pltpu.VMEM((CK, ROWS), bf16), pltpu.VMEM((CK, ROWS), bf16),
           pltpu.SemaphoreType.DMA((sems,)), pltpu.SemaphoreType.DMA((sems,)), pltpu.SemaphoreType.DMA((2,))],
        compiler_params=pltpu.CompilerParams(collective_id=0, has_side_effects=True, vmem_limit_bytes=62 * 2**20),
        name="shared",
    )(loc, held_block, resp_prompt, resp_len, queries, grad_out, resp_kv, prefix_kv)


def solution(mesh):
    rows = P("dp", None)
    return jax.shard_map(on_device, mesh=mesh, in_specs=(rows, rows, rows, rows, P(), P(), P()),
                         out_specs=(rows, rows, rows, rows), check_vma=False)
```

```python
import math

import jax
import jax.numpy as jnp
from jax import lax
from jax.experimental import pallas as pl
from jax.experimental.pallas import tpu as pltpu
from jax.sharding import PartitionSpec as P

f32, bf16 = jnp.float32, jnp.bfloat16
MESH = pl.DeviceIdType.MESH
NN = (((1,), (0,)), ((), ()))
SIDE = 4
D = 128
HEADS = 8
ROWS = 512
BLOCKS = 32
CHUNKS = 4
CK = 512
PK = CHUNKS * CK
NK = PK + ROWS
HALF = ROWS // 2
UNROLL = 4
SCALE = 1.0 / math.sqrt(D)
LOG2 = SCALE * math.log2(math.e)
ORDERS = ((0, 1, 2), (1, 2, 0), (2, 0, 1))
HOPS = (2, 1, 3)
PARTS = [(c, t) for c in range(CHUNKS) for t in range(2)]


def mm(a, b):
    return lax.dot_general(a, b, NN, preferred_element_type=f32)


def place():
    me = lax.axis_index("dp")
    return (me // 32, me // 8 % SIDE, me // 2 % SIDE), me % 2


def device(at, core):
    return ((at[0] * SIDE + at[1]) * SIDE + at[2]) * 2 + core


def moved(at, axis, step):
    return tuple((c + step) % SIDE if a == axis else c for a, c in enumerate(at))


class Sender:
    def __init__(self, send, recv):
        self.send, self.recv, self.count, self.all = send, recv, 0, []

    def __call__(self, src, dst, to):
        c = self.ready(src, dst, to)
        c.start()
        return c

    def ready(self, src, dst, to):
        i = self.count
        self.count += 1
        c = pltpu.make_async_remote_copy(src_ref=src, dst_ref=dst, send_sem=self.send.at[i], recv_sem=self.recv.at[i],
                                         device_id=(to,), device_id_type=MESH)
        self.all.append(c)
        return c

    def drain(self):
        for c in self.all:
            c.wait_send()


class Gather:
    def __init__(self, go, at, core, refs, stages):
        self.go, self.at, self.core, self.refs, self.stages = go, at, core, refs, stages
        self.flying = {}

    def put(self, x_ref):
        for n, (c, t) in enumerate(PARTS):
            a, b, _ = ORDERS[n % 3]
            self.stages[n % 3][self.at[a], self.at[b], n // 3] = x_ref[16 * c:16 * c + 16, D * t:D * t + D]

    def start(self, k, i):
        a, b, _ = ORDERS[k]
        v = self.stages[k].at[self.at[a], self.at[b]] if i == 0 else self.stages[k].at[:, self.at[b]]
        self.flying[k, i] = [self.go(v, v, device(moved(self.at, ORDERS[k][i], s), self.core)) for s in HOPS]

    def start_last(self, n):
        a = ORDERS[n % 3][2]
        src, dst = self.stages[n % 3].at[:, :, n // 3], self.refs[n].at[self.core, self.at[a]]
        self.flying["part", n] = [self.go(src, dst, device(moved(self.at, a, s), self.core)) for s in HOPS]
        self.refs[n][self.core, self.at[a]] = self.stages[n % 3][:, :, n // 3]

    def wait(self, *key):
        for c in self.flying[key]:
            c.wait_recv()

    def start_core(self, n):
        v = self.refs[n].at[self.core]
        self.flying["core", n] = [self.go(v, v, device(self.at, 1 - self.core))]


class Scatter:
    def __init__(self, go, at, core, held, prompt, own, peer, w, bufs, out):
        self.go, self.at, self.core, self.held, self.prompt = go, at, core, held, prompt
        self.own, self.peer, self.w, self.bufs, self.out = own, peer, w, bufs, out
        self.flying = {}
        self.coord = [[(at[a] + s) % SIDE for s in HOPS] for a in range(3)]
        self.dev = [[device(moved(at, a, s), core) for s in HOPS] for a in range(3)]
        self.other_core = device(at, 1 - core)

    def swap(self, c):
        self.flying[c] = self.go(self.own[c], self.peer[c], self.other_core)

    def fill(self, c):
        self.flying[c].wait_recv()
        mine = self.prompt[device(self.at, self.core)]
        other = self.prompt[device(self.at, 1 - self.core)]
        own, peer, w = self.own[c], self.peer[c], self.w[c]
        zero = jnp.zeros((32, D), bf16)

        def body(j, _):
            for u in range(4):
                b = self.held[(j * 4 + u) * 2 + self.core]
                p, k = lax.shift_right_logical(b, 5), lax.bitwise_and(b, 31)
                w[j // 4, j % 4, u] = jnp.where(p == mine, own[k], zero) + jnp.where(p == other, peer[k], zero)
            return 0

        lax.fori_loop(0, 16, body, 0)

    def spot(self, n, i, k):
        c, t = PARTS[n]
        order = ORDERS[n % 3]
        idx = [self.at[a] if a in order[:i] else k if a == order[i] else slice(0, SIDE) for a in range(3)]
        return (*idx, slice(16 * t, 16 * t + 16), slice(None))

    def ready(self, c, i):
        for n in (2 * c, 2 * c + 1):
            a = ORDERS[n % 3][i]
            self.flying[n, i] = [
                self.go.ready(self.w[c].at[self.spot(n, i, self.coord[a][j])], self.bufs[3 * n + i].at[j], self.dev[a][j])
                for j in range(3)]

    def start(self, c, i):
        if (2 * c, i) not in self.flying:
            self.ready(c, i)
        for n in (2 * c, 2 * c + 1):
            for f in self.flying[n, i]:
                f.start()

    def add(self, c, i):
        for n in (2 * c, 2 * c + 1):
            for f in self.flying[n, i]:
                f.wait_recv()
            buf = self.bufs[3 * n + i]
            here = self.spot(n, i, self.at[ORDERS[n % 3][i]])
            total = (self.w[c][here].astype(f32) + buf[0].astype(f32)) + (buf[1].astype(f32) + buf[2].astype(f32))
            if i < 2:
                self.w[c][here] = total.astype(bf16)
            else:
                t = n % 2
                self.out[16 * c:16 * c + 16, D * t:D * t + D] = total

    def stage(self, c, s):
        if s == 0:
            self.fill(c)
            self.start(c, 0)
        else:
            self.add(c, s - 1)
            if s < 3:
                self.start(c, s)


def kernel(loc_ref, held_ref, prompt_ref, len_ref, q_hbm, g_hbm, rkv_ref, x_ref, o_hbm, dq_hbm, drkv_hbm, out_ref, *rest):
    gref, stages, rest = rest[:8], rest[8:11], rest[11:]
    own, peer, w, bufs, rest = rest[:4], rest[4:8], rest[8:12], rest[12:36], rest[36:]
    q_ref, g_ref, kk, vv, kt, vt, q2t, g2t, gp, e_all, ms, ls, ot, o_ref, dq_ref, drkv_ref, dk, dv, s0, s1, p0, p1, send, recv, local = rest
    at, core = place()
    me = device(at, core)
    barrier = pltpu.get_barrier_semaphore()
    near = [device(moved(at, a, s), core) for a in range(3) for s in HOPS] + [device(at, 1 - core)]
    for n in near:
        pl.semaphore_signal(barrier, inc=1, device_id=(n,), device_id_type=MESH)
    q_in = pltpu.make_async_copy(q_hbm, q_ref, local.at[0])
    g_in = pltpu.make_async_copy(g_hbm, g_ref, local.at[1])
    q_in.start()
    g_in.start()
    go = Sender(send, recv)
    gather = Gather(go, at, core, gref, stages)
    gather.put(x_ref)
    pl.semaphore_wait(barrier, len(near))
    for k in range(3):
        gather.start(k, 0)

    length = len_ref[me]
    live = lax.broadcasted_iota(jnp.int32, (1, ROWS), 1) < length
    tri = lax.broadcasted_iota(jnp.int32, (HALF, HALF), 0) <= lax.broadcasted_iota(jnp.int32, (HALF, HALF), 1)
    vv[:, D:] = jnp.ones((NK, D), bf16)

    def heads_loop(lo, hi, item, step=UNROLL):
        def body(i, _):
            for u in range(step):
                item(i * step + u)
            return 0
        lax.fori_loop(lo // step, hi // step, body, 0)

    def staged(ahead, item, slots, middle=None):
        slots[0][...] = ahead(0)

        def body(i, _):
            if middle is not None:
                pl.when(i == 1)(middle)
            for u in range(UNROLL):
                h = i * UNROLL + u
                slots[(u + 1) % 2][...] = ahead(lax.rem(h + 1, HEADS))
                item(h, slots[u % 2])
            return 0
        lax.fori_loop(0, HEADS // UNROLL, body, 0)

    def cols(h):
        return pl.ds(pl.multiple_of(h * D, D), D)

    def prepare(h):
        qs = q_ref[:, cols(h)].astype(f32) * LOG2
        hi = qs.astype(bf16)
        lo = (qs - hi.astype(f32)).astype(bf16)
        q2t[h, 0:D] = hi.T
        q2t[h, D:] = lo.T

    def place_keys(k0, kn, keys, vals):
        kk[k0:k0 + kn, 0:D] = keys
        kk[k0:k0 + kn, D:] = keys
        vv[k0:k0 + kn, 0:D] = vals

    def turn(k0, kn):
        kt[:, k0:k0 + kn] = kk[k0:k0 + kn, 0:D].T
        vt[:, k0:k0 + kn] = vv[k0:k0 + kn, 0:D].T

    def first(h):
        sa = mm(kk[PK:PK + HALF, :], q2t[h])
        sa = jnp.concatenate([jnp.where(tri, sa[:, :HALF], -1e30), sa[:, HALF:]], axis=1)
        sb = jnp.where(tri, mm(kk[PK + HALF:, :], q2t[h, :, HALF:]), -1e30)
        m = jnp.max(sa, axis=0, keepdims=True)
        m = jnp.concatenate([m[:, :HALF], jnp.maximum(m[:, HALF:], jnp.max(sb, axis=0, keepdims=True))], axis=1)
        ea = jnp.exp2(sa - m)
        eb = jnp.exp2(sb - m[:, HALF:])
        l = jnp.sum(ea, axis=0, keepdims=True)
        l = jnp.concatenate([l[:, :HALF], l[:, HALF:] + jnp.sum(eb, axis=0, keepdims=True)], axis=1)
        ea, eb = ea.astype(bf16), eb.astype(bf16)
        e_all[h, PK:PK + HALF, :] = ea
        e_all[h, PK + HALF:, HALF:] = eb
        oa = mm(vt[:, PK:PK + HALF], ea)
        ob = mm(vt[:, PK + HALF:], eb)
        ms[0, h] = m
        ls[h] = l
        ot[h, :, 0:HALF] = oa[:, :HALF]
        ot[h, :, HALF:] = oa[:, HALF:] + ob

    def forward(c):
        k0 = c * CK

        def ahead(h):
            return mm(kk[k0:k0 + CK, :], q2t[h])

        def item(h, s):
            old = ms[c, h]
            m = jnp.maximum(old, jnp.max(s[...], axis=0, keepdims=True))
            e = jnp.exp2(s[...] - m)
            fade = jnp.exp2(old - m)
            ls[h] = ls[h] * fade + jnp.sum(e, axis=0, keepdims=True)
            e = e.astype(bf16)
            e_all[h, k0:k0 + CK, :] = e
            ot[h] = ot[h] * fade + mm(vt[:, k0:k0 + CK], e)
            ms[c + 1, h] = m
        staged(ahead, item, (s0, s1))

    def finish(h):
        f = jnp.where(live, 1.0 / ls[h], 0.0)
        o = ot[h] * f
        ot[h] = o
        gt = g_ref[:, cols(h)].T.astype(f32)
        gt = jnp.where(live, gt, 0.0) * f
        neg = -jnp.sum(gt * o, axis=0, keepdims=True)
        gb = gt.astype(bf16)
        gp[h] = gb.T
        hi = neg.astype(bf16).astype(f32)
        sub = lax.broadcasted_iota(jnp.int32, (16, ROWS), 0)
        extra = jnp.where(sub == 0, hi, jnp.where(sub == 1, neg - hi, 0.0)).astype(bf16)
        g2t[h, 0:D] = gb
        g2t[h, D:D + 16] = extra
        g2t[h, D + 16:] = jnp.zeros((D - 16, ROWS), bf16)

    def slope(h, k0, kn, r0):
        return mm(vv[k0:k0 + kn, :], g2t[h, :, r0:]).astype(bf16)

    def back(h, dp, k0, kn, r0, stage, a0):
        fade = jnp.exp2(ms[stage, h] - ms[CHUNKS, h]).astype(bf16)[:, r0:]
        e = e_all[h, k0:k0 + kn, r0:] * fade
        ds = e * dp
        e_all[h, k0:k0 + kn, r0:] = ds
        dk[a0:a0 + kn, :] += mm(ds, q_ref[r0:, cols(h)])
        dv[a0:a0 + kn, :] += mm(e, gp[h, r0:, :])

    def load_chunk(c):
        for n in (2 * c, 2 * c + 1):
            gather.wait("core", n)
        prompt = prompt_ref[me]
        for b in range(BLOCKS):
            n = loc_ref[prompt * BLOCKS + b]
            held_at = (lax.shift_right_logical(n, 5), lax.bitwise_and(lax.shift_right_logical(n, 3), 3),
                       lax.bitwise_and(lax.shift_right_logical(n, 1), 3))
            keys, vals = [gref[p][(lax.bitwise_and(n, 1),) + tuple(held_at[ORDERS[p % 3][i]] for i in (2, 0, 1))]
                          for p in (2 * c, 2 * c + 1)]
            place_keys(c * CK + 16 * b, 16, keys, vals)
        turn(c * CK, CK)

    place_keys(PK, ROWS, rkv_ref[:, 0:D], rkv_ref[:, D:])
    turn(PK, ROWS)
    q_in.wait()
    heads_loop(0, HEADS, prepare)
    for k in range(3):
        gather.wait(k, 0)
        gather.start(k, 1)
    heads_loop(0, 4, first)
    for k in range(3):
        gather.wait(k, 1)
    for n in range(8):
        gather.start_last(n)
    heads_loop(4, HEADS, first)

    def pass_on(c):
        for n in (2 * c, 2 * c + 1):
            gather.wait("part", n)
            gather.start_core(n)

    pass_on(0)
    for c in range(CHUNKS):
        load_chunk(c)
        if c + 1 < CHUNKS:
            pass_on(c + 1)
        forward(c)
    g_in.wait()
    heads_loop(0, HEADS, finish)

    scatter = Scatter(go, at, core, held_ref, prompt_ref, own, peer, w, bufs, out_ref)
    for c in range(CHUNKS):
        dk[...] = jnp.zeros_like(dk)
        dv[...] = jnp.zeros_like(dv)
        middle = None
        if c:
            scatter.ready(c - 1, 0)
            middle = lambda: scatter.stage(c - 1, 0)
        staged(lambda h: slope(h, c * CK, CK, 0), lambda h, dp: back(h, dp[...], c * CK, CK, 0, c + 1, 0), (p0, p1), middle)
        own[c][:, 0:16, :] = (dk[...] * SCALE).astype(bf16).reshape(BLOCKS, 16, D)
        own[c][:, 16:, :] = dv[...].astype(bf16).reshape(BLOCKS, 16, D)
        scatter.swap(c)
        if c >= 2:
            scatter.stage(c - 2, 1)
    scatter.stage(0, 2)
    dk[...] = jnp.zeros_like(dk)
    dv[...] = jnp.zeros_like(dv)

    def last(h):
        back(h, slope(h, PK, HALF, 0), PK, HALF, 0, 0, 0)
        back(h, slope(h, PK + HALF, HALF, HALF), PK + HALF, HALF, HALF, 0, HALF)

    def rows_out(h):
        dq_ref[:HALF, cols(h)] = (mm(kt[:, :PK + HALF], e_all[h, :PK + HALF, :HALF]) * SCALE).astype(bf16).T
        dq_ref[HALF:, cols(h)] = (mm(kt[...], e_all[h, :, HALF:]) * SCALE).astype(bf16).T
        o_ref[:, cols(h)] = ot[h].astype(bf16).T

    def send_home(src, dst, i):
        c = pltpu.make_async_copy(src, dst, local.at[i])
        c.start()
        return c

    heads_loop(0, 4, last)
    scatter.stage(3, 0)
    scatter.stage(2, 1)
    scatter.stage(1, 2)
    scatter.stage(0, 3)
    heads_loop(4, HEADS, last)
    drkv_ref[:, 0:D] = (dk[...] * SCALE).astype(bf16)
    drkv_ref[:, D:] = dv[...].astype(bf16)
    home = [send_home(drkv_ref, drkv_hbm, 2)]
    heads_loop(0, 4, rows_out)
    half = HEADS * D // 2
    home.append(send_home(o_ref.at[:, :half], o_hbm.at[:, :half], 3))
    home.append(send_home(dq_ref.at[:, :half], dq_hbm.at[:, :half], 4))
    scatter.stage(2, 2)
    scatter.stage(1, 3)
    scatter.stage(3, 1)
    heads_loop(4, HEADS, rows_out)
    home.append(send_home(o_ref.at[:, half:], o_hbm.at[:, half:], 5))
    home.append(send_home(dq_ref.at[:, half:], dq_hbm.at[:, half:], 6))
    scatter.stage(2, 3)
    scatter.stage(3, 2)
    scatter.stage(3, 3)
    for c in home:
        c.wait()
    go.drain()


def on_device(queries, resp_kv, prefix_kv, grad_out, held_block, resp_prompt, resp_len):
    spots = jnp.arange(128, dtype=jnp.int32)
    loc = jnp.sum(jnp.where(held_block[None, :] == spots[:, None], spots[None, :], 0), axis=1).astype(jnp.int32)
    bufs = []
    for n in range(8):
        for i in range(3):
            bufs.append(pltpu.VMEM((3,) + (SIDE,) * (2 - i) + (16, D), bf16))
    sm = pl.BlockSpec(memory_space=pltpu.SMEM)
    vm = pl.BlockSpec(memory_space=pltpu.VMEM)
    hbm = pl.BlockSpec(memory_space=pl.ANY)
    sems = 18 + 8 * 4 + 8 * 9 + 4
    outs = pl.pallas_call(
        kernel,
        out_shape=(jax.ShapeDtypeStruct(queries.shape, bf16), jax.ShapeDtypeStruct(queries.shape, bf16),
                   jax.ShapeDtypeStruct(resp_kv.shape, bf16), jax.ShapeDtypeStruct((64, 256), f32)),
        in_specs=[sm] * 4 + [hbm] * 2 + [vm] * 2,
        out_specs=(hbm,) * 3 + (vm,),
        scratch_shapes=[pltpu.VMEM((2, SIDE, SIDE, SIDE, 16, D), bf16)] * 8
        + [pltpu.VMEM((SIDE, SIDE, k, 16, D), bf16) for k in (3, 3, 2)]
        + [pltpu.VMEM((BLOCKS, 32, D), bf16)] * 8 + [pltpu.VMEM((SIDE, SIDE, SIDE, 32, D), bf16)] * 4 + bufs
        + [pltpu.VMEM((ROWS, HEADS * D), bf16), pltpu.VMEM((ROWS, HEADS * D), bf16),
           pltpu.VMEM((NK, 2 * D), bf16), pltpu.VMEM((NK, 2 * D), bf16), pltpu.VMEM((D, NK), bf16),
           pltpu.VMEM((D, NK), bf16), pltpu.VMEM((HEADS, 2 * D, ROWS), bf16), pltpu.VMEM((HEADS, 2 * D, ROWS), bf16),
           pltpu.VMEM((HEADS, ROWS, D), bf16), pltpu.VMEM((HEADS, NK, ROWS), bf16),
           pltpu.VMEM((CHUNKS + 1, HEADS, 1, ROWS), f32), pltpu.VMEM((HEADS, 1, ROWS), f32),
           pltpu.VMEM((HEADS, D, ROWS), f32), pltpu.VMEM((ROWS, HEADS * D), bf16), pltpu.VMEM((ROWS, HEADS * D), bf16),
           pltpu.VMEM((ROWS, 2 * D), bf16),
           pltpu.VMEM((ROWS, D), f32), pltpu.VMEM((ROWS, D), f32),
           pltpu.VMEM((CK, ROWS), f32), pltpu.VMEM((CK, ROWS), f32), pltpu.VMEM((CK, ROWS), bf16), pltpu.VMEM((CK, ROWS), bf16),
           pltpu.SemaphoreType.DMA((sems,)), pltpu.SemaphoreType.DMA((sems,)), pltpu.SemaphoreType.DMA((7,))],
        compiler_params=pltpu.CompilerParams(collective_id=0, has_side_effects=True, vmem_limit_bytes=62 * 2**20),
        name="shared",
    )(loc, held_block, resp_prompt, resp_len, queries, grad_out, resp_kv, prefix_kv)
    return deliver(outs)


def deliver_kernel(*refs):
    n = len(refs) // 3
    sems = refs[-1]
    moves = []
    for i in range(n):
        src, dst, held = refs[i], refs[n + i], refs[2 * n + i]
        pieces = 4 if i < 2 else 1
        size = src.shape[0] // pieces
        for p in range(pieces):
            rows, k = slice(p * size, p * size + size), len(moves)
            moves.append((pltpu.make_async_copy(src.at[rows], held.at[rows], sems.at[0, k]),
                          pltpu.make_async_copy(held.at[rows], dst.at[rows], sems.at[1, k])))
    for bring, _ in moves:
        bring.start()
    for bring, leave in moves:
        bring.wait()
        leave.start()
    for _, leave in moves:
        leave.wait()


def deliver(arrays):
    hbm = pl.BlockSpec(memory_space=pl.ANY)
    return pl.pallas_call(
        deliver_kernel,
        out_shape=tuple(jax.ShapeDtypeStruct(a.shape, a.dtype) for a in arrays),
        in_specs=[hbm] * len(arrays),
        out_specs=(hbm,) * len(arrays),
        scratch_shapes=[pltpu.VMEM(a.shape, a.dtype) for a in arrays] + [pltpu.SemaphoreType.DMA((2, 10))],
        compiler_params=pltpu.CompilerParams(vmem_limit_bytes=62 * 2**20),
        name="deliver",
    )(*arrays)


def solution(mesh):
    rows = P("dp", None)
    return jax.shard_map(on_device, mesh=mesh, in_specs=(rows, rows, rows, rows, P(), P(), P()),
                         out_specs=(rows, rows, rows, rows), check_vma=False)
```

```python
import math

import jax
import jax.numpy as jnp
from jax import lax
from jax.experimental import pallas as pl
from jax.experimental.pallas import tpu as pltpu
from jax.sharding import PartitionSpec as P

f32, bf16 = jnp.float32, jnp.bfloat16
MESH = pl.DeviceIdType.MESH
NN = (((1,), (0,)), ((), ()))
SIDE = 4
D = 128
HEADS = 8
ROWS = 512
BLOCKS = 32
CHUNKS = 4
CK = 512
PK = CHUNKS * CK
NK = PK + ROWS
HALF = ROWS // 2
UNROLL = 4
SCALE = 1.0 / math.sqrt(D)
LOG2 = SCALE * math.log2(math.e)
ORDERS = ((0, 1, 2), (1, 2, 0), (2, 0, 1))
HOPS = (2, 1, 3)
PARTS = [(c, t) for c in range(CHUNKS) for t in range(2)]


def mm(a, b):
    return lax.dot_general(a, b, NN, preferred_element_type=f32)


def place():
    me = lax.axis_index("dp")
    return (me // 32, me // 8 % SIDE, me // 2 % SIDE), me % 2


def device(at, core):
    return ((at[0] * SIDE + at[1]) * SIDE + at[2]) * 2 + core


def moved(at, axis, step):
    return tuple((c + step) % SIDE if a == axis else c for a, c in enumerate(at))


class Sender:
    def __init__(self, send, recv):
        self.send, self.recv, self.count, self.all = send, recv, 0, []

    def __call__(self, src, dst, to):
        c = self.ready(src, dst, to)
        c.start()
        return c

    def ready(self, src, dst, to):
        i = self.count
        self.count += 1
        c = pltpu.make_async_remote_copy(src_ref=src, dst_ref=dst, send_sem=self.send.at[i], recv_sem=self.recv.at[i],
                                         device_id=(to,), device_id_type=MESH)
        self.all.append(c)
        return c

    def drain(self):
        for c in self.all:
            c.wait_send()


class Gather:
    def __init__(self, go, at, core, refs, stages):
        self.go, self.at, self.core, self.refs, self.stages = go, at, core, refs, stages
        self.flying = {}

    def put(self, x_ref):
        for n, (c, t) in enumerate(PARTS):
            a, b, _ = ORDERS[n % 3]
            self.stages[n % 3][self.at[a], self.at[b], n // 3] = x_ref[16 * c:16 * c + 16, D * t:D * t + D]

    def start(self, k, i):
        a, b, _ = ORDERS[k]
        v = self.stages[k].at[self.at[a], self.at[b]] if i == 0 else self.stages[k].at[:, self.at[b]]
        self.flying[k, i] = [self.go(v, v, device(moved(self.at, ORDERS[k][i], s), self.core)) for s in HOPS]

    def start_last(self, n):
        a = ORDERS[n % 3][2]
        src, dst = self.stages[n % 3].at[:, :, n // 3], self.refs[n].at[self.core, self.at[a]]
        self.flying["part", n] = [self.go(src, dst, device(moved(self.at, a, s), self.core)) for s in HOPS]
        self.refs[n][self.core, self.at[a]] = self.stages[n % 3][:, :, n // 3]

    def wait(self, *key):
        for c in self.flying[key]:
            c.wait_recv()

    def pass_on(self, n):
        p, to = self.at[ORDERS[n % 3][2]], device(self.at, 1 - self.core)
        self.flying["core", n] = []
        for near in (None, 1, 2, 0):
            k = p
            if near is not None:
                self.flying["part", n][near].wait_recv()
                k = (p + SIDE - HOPS[near]) % SIDE
            v = self.refs[n].at[self.core, k]
            self.flying["core", n].append(self.go(v, v, to))


class Scatter:
    def __init__(self, go, at, core, held, prompt, own, peer, w, bufs, out):
        self.go, self.at, self.core, self.held, self.prompt = go, at, core, held, prompt
        self.own, self.peer, self.w, self.bufs, self.out = own, peer, w, bufs, out
        self.flying = {}
        self.coord = [[(at[a] + s) % SIDE for s in HOPS] for a in range(3)]
        self.dev = [[device(moved(at, a, s), core) for s in HOPS] for a in range(3)]
        self.other_core = device(at, 1 - core)

    def swap(self, c):
        self.flying[c] = self.go(self.own[c], self.peer[c], self.other_core)

    def fill(self, c):
        self.flying[c].wait_recv()
        mine = self.prompt[device(self.at, self.core)]
        other = self.prompt[device(self.at, 1 - self.core)]
        own, peer, w = self.own[c], self.peer[c], self.w[c]
        zero = jnp.zeros((32, D), bf16)

        def body(j, _):
            for u in range(4):
                b = self.held[(j * 4 + u) * 2 + self.core]
                p, k = lax.shift_right_logical(b, 5), lax.bitwise_and(b, 31)
                w[j // 4, j % 4, u] = jnp.where(p == mine, own[k], zero) + jnp.where(p == other, peer[k], zero)
            return 0

        lax.fori_loop(0, 16, body, 0)

    def spot(self, n, i, k):
        c, t = PARTS[n]
        order = ORDERS[n % 3]
        idx = [self.at[a] if a in order[:i] else k if a == order[i] else slice(0, SIDE) for a in range(3)]
        return (*idx, slice(16 * t, 16 * t + 16), slice(None))

    def ready(self, c, i):
        for n in (2 * c, 2 * c + 1):
            a = ORDERS[n % 3][i]
            self.flying[n, i] = [
                self.go.ready(self.w[c].at[self.spot(n, i, self.coord[a][j])], self.bufs[3 * n + i].at[j], self.dev[a][j])
                for j in range(3)]

    def start(self, c, i):
        if (2 * c, i) not in self.flying:
            self.ready(c, i)
        for n in (2 * c, 2 * c + 1):
            for f in self.flying[n, i]:
                f.start()

    def add(self, c, i):
        for n in (2 * c, 2 * c + 1):
            for f in self.flying[n, i]:
                f.wait_recv()
            buf = self.bufs[3 * n + i]
            here = self.spot(n, i, self.at[ORDERS[n % 3][i]])
            total = (self.w[c][here].astype(f32) + buf[0].astype(f32)) + (buf[1].astype(f32) + buf[2].astype(f32))
            if i < 2:
                self.w[c][here] = total.astype(bf16)
            else:
                t = n % 2
                self.out[16 * c:16 * c + 16, D * t:D * t + D] = total

    def stage(self, c, s):
        if s == 0:
            self.fill(c)
            self.start(c, 0)
        else:
            self.add(c, s - 1)
            if s < 3:
                self.start(c, s)


def kernel(held_vec, held_ref, prompt_ref, len_ref, q_hbm, g_hbm, rkv_ref, x_ref, o_hbm, dq_hbm, drkv_hbm, out_ref, *rest):
    gref, stages, rest = rest[:8], rest[8:11], rest[11:]
    own, peer, w, bufs, rest = rest[:4], rest[4:8], rest[8:12], rest[12:36], rest[36:]
    q_ref, g_ref, kk, vv, kt, vt, q2t, g2t, gp, e_all, loc_ref, ms, ls, ot, o_ref, dq_ref, drkv_ref, dk, dv, s0, s1, p0, p1, send, recv, local = rest
    at, core = place()
    me = device(at, core)
    barrier = pltpu.get_barrier_semaphore()
    near = [device(moved(at, a, s), core) for a in range(3) for s in HOPS] + [device(at, 1 - core)]
    for n in near:
        pl.semaphore_signal(barrier, inc=1, device_id=(n,), device_id_type=MESH)
    q_in = pltpu.make_async_copy(q_hbm, q_ref, local.at[0])
    g_in = pltpu.make_async_copy(g_hbm, g_ref, local.at[1])
    q_in.start()
    g_in.start()
    go = Sender(send, recv)
    gather = Gather(go, at, core, gref, stages)
    gather.put(x_ref)
    pl.semaphore_wait(barrier, len(near))
    for k in range(3):
        gather.start(k, 0)

    length = len_ref[me]
    live = lax.broadcasted_iota(jnp.int32, (1, ROWS), 1) < length
    tri = lax.broadcasted_iota(jnp.int32, (HALF, HALF), 0) <= lax.broadcasted_iota(jnp.int32, (HALF, HALF), 1)
    vv[:, D:] = jnp.ones((NK, D), bf16)

    def heads_loop(lo, hi, item, step=UNROLL):
        def body(i, _):
            for u in range(step):
                item(i * step + u)
            return 0
        lax.fori_loop(lo // step, hi // step, body, 0)

    def staged(ahead, item, slots):
        slots[0][...] = ahead(0)

        def body(i, _):
            for u in range(UNROLL):
                h = i * UNROLL + u
                slots[(u + 1) % 2][...] = ahead(lax.rem(h + 1, HEADS))
                item(h, slots[u % 2])
            return 0
        lax.fori_loop(0, HEADS // UNROLL, body, 0)

    def straight(ahead, item, slots, middle):
        slots[0][...] = ahead(0)
        for h in range(HEADS):
            if h == HEADS // 2:
                for job in middle:
                    scatter.stage(*job)
            if h + 1 < HEADS:
                slots[(h + 1) % 2][...] = ahead(h + 1)
            item(h, slots[h % 2])

    def cols(h):
        if isinstance(h, int):
            return slice(h * D, h * D + D)
        return pl.ds(pl.multiple_of(h * D, D), D)

    def prepare(h):
        qs = q_ref[:, cols(h)].astype(f32) * LOG2
        hi = qs.astype(bf16)
        lo = (qs - hi.astype(f32)).astype(bf16)
        q2t[h, 0:D] = hi.T
        q2t[h, D:] = lo.T
        g2t[h, 0:D] = g_ref[:, cols(h)].T
        g2t[h, D + 16:] = jnp.zeros((D - 16, ROWS), bf16)

    def place_keys(k0, kn, keys, vals):
        kk[k0:k0 + kn, 0:D] = keys
        kk[k0:k0 + kn, D:] = keys
        vv[k0:k0 + kn, 0:D] = vals

    def turn(k0, kn):
        kt[:, k0:k0 + kn] = kk[k0:k0 + kn, 0:D].T
        vt[:, k0:k0 + kn] = vv[k0:k0 + kn, 0:D].T

    def first(h):
        sa = mm(kk[PK:PK + HALF, :], q2t[h])
        sa = jnp.concatenate([jnp.where(tri, sa[:, :HALF], -1e30), sa[:, HALF:]], axis=1)
        sb = jnp.where(tri, mm(kk[PK + HALF:, :], q2t[h, :, HALF:]), -1e30)
        m = jnp.max(sa, axis=0, keepdims=True)
        m = jnp.concatenate([m[:, :HALF], jnp.maximum(m[:, HALF:], jnp.max(sb, axis=0, keepdims=True))], axis=1)
        ea = jnp.exp2(sa - m)
        eb = jnp.exp2(sb - m[:, HALF:])
        l = jnp.sum(ea, axis=0, keepdims=True)
        l = jnp.concatenate([l[:, :HALF], l[:, HALF:] + jnp.sum(eb, axis=0, keepdims=True)], axis=1)
        ea, eb = ea.astype(bf16), eb.astype(bf16)
        e_all[h, PK:PK + HALF, :] = ea
        e_all[h, PK + HALF:, HALF:] = eb
        oa = mm(vt[:, PK:PK + HALF], ea)
        ob = mm(vt[:, PK + HALF:], eb)
        ms[0, h] = m
        ls[h] = l
        ot[h, :, 0:HALF] = oa[:, :HALF]
        ot[h, :, HALF:] = oa[:, HALF:] + ob

    def forward(c):
        k0 = c * CK

        def ahead(h):
            return mm(kk[k0:k0 + CK, :], q2t[h])

        def item(h, s):
            old = ms[c, h]
            m = jnp.maximum(old, jnp.max(s[...], axis=0, keepdims=True))
            e = jnp.exp2(s[...] - m)
            fade = jnp.exp2(old - m)
            ls[h] = ls[h] * fade + jnp.sum(e, axis=0, keepdims=True)
            e = e.astype(bf16)
            e_all[h, k0:k0 + CK, :] = e
            ot[h] = ot[h] * fade + mm(vt[:, k0:k0 + CK], e)
            ms[c + 1, h] = m
        staged(ahead, item, (s0, s1))

    def finish(h):
        f = jnp.where(live, 1.0 / ls[h], 0.0)
        o = ot[h] * f
        ot[h] = o
        gt = g2t[h, 0:D].astype(f32)
        gt = jnp.where(live, gt, 0.0) * f
        neg = -jnp.sum(gt * o, axis=0, keepdims=True)
        gb = gt.astype(bf16)
        gp[h] = gb.T
        hi = neg.astype(bf16).astype(f32)
        sub = lax.broadcasted_iota(jnp.int32, (16, ROWS), 0)
        extra = jnp.where(sub == 0, hi, jnp.where(sub == 1, neg - hi, 0.0)).astype(bf16)
        g2t[h, 0:D] = gb
        g2t[h, D:D + 16] = extra

    def slope(h, k0, kn, r0):
        return mm(vv[k0:k0 + kn, :], g2t[h, :, r0:]).astype(bf16)

    def back(h, dp, k0, kn, r0, stage, a0):
        fade = jnp.exp2(ms[stage, h] - ms[CHUNKS, h]).astype(bf16)[:, r0:]
        e = e_all[h, k0:k0 + kn, r0:] * fade
        ds = e * dp
        e_all[h, k0:k0 + kn, r0:] = ds
        dk[a0:a0 + kn, :] += mm(ds, q_ref[r0:, cols(h)])
        dv[a0:a0 + kn, :] += mm(e, gp[h, r0:, :])

    def load_chunk(c):
        for n in (2 * c, 2 * c + 1):
            gather.wait("core", n)
        for b in range(BLOCKS):
            n = loc_ref[b]
            held_at = (lax.shift_right_logical(n, 5), lax.bitwise_and(lax.shift_right_logical(n, 3), 3),
                       lax.bitwise_and(lax.shift_right_logical(n, 1), 3))
            keys, vals = [gref[p][(lax.bitwise_and(n, 1),) + tuple(held_at[ORDERS[p % 3][i]] for i in (2, 0, 1))]
                          for p in (2 * c, 2 * c + 1)]
            place_keys(c * CK + 16 * b, 16, keys, vals)
        turn(c * CK, CK)

    place_keys(PK, ROWS, rkv_ref[:, 0:D], rkv_ref[:, D:])
    turn(PK, ROWS)
    q_in.wait()
    g_in.wait()
    heads_loop(0, HEADS, prepare)
    for k in range(3):
        gather.wait(k, 0)
        gather.start(k, 1)
    heads_loop(0, 4, first)
    for k in range(3):
        gather.wait(k, 1)
    for n in range(8):
        gather.start_last(n)
    heads_loop(4, HEADS, first)

    lane = lax.broadcasted_iota(jnp.int32, (1, 128), 1)
    held_row = held_vec[...].reshape(1, 128)
    base = prompt_ref[me] * BLOCKS
    for b in range(BLOCKS):
        loc_ref[b] = jnp.max(jnp.where(held_row == base + b, lane, 0))

    def pass_on(c):
        for n in (2 * c, 2 * c + 1):
            gather.pass_on(n)

    pass_on(0)
    for c in range(CHUNKS):
        load_chunk(c)
        if c + 1 < CHUNKS:
            pass_on(c + 1)
        forward(c)
    heads_loop(0, HEADS, finish)

    scatter = Scatter(go, at, core, held_ref, prompt_ref, own, peer, w, bufs, out_ref)
    for c in range(CHUNKS):
        dk[...] = jnp.zeros_like(dk)
        dv[...] = jnp.zeros_like(dv)
        middle = [] if c == 0 else [(c - 1, 0)] if c < 3 else [(2, 0), (0, 1)]
        straight(lambda h: slope(h, c * CK, CK, 0), lambda h, dp: back(h, dp[...], c * CK, CK, 0, c + 1, 0), (p0, p1), middle)
        own[c][:, 0:16, :] = (dk[...] * SCALE).astype(bf16).reshape(BLOCKS, 16, D)
        own[c][:, 16:, :] = dv[...].astype(bf16).reshape(BLOCKS, 16, D)
        scatter.swap(c)
    dk[...] = jnp.zeros_like(dk)
    dv[...] = jnp.zeros_like(dv)

    def last(h):
        back(h, slope(h, PK, HALF, 0), PK, HALF, 0, 0, 0)
        back(h, slope(h, PK + HALF, HALF, HALF), PK + HALF, HALF, HALF, 0, HALF)

    def rows_out(h):
        dq_ref[:HALF, cols(h)] = (mm(kt[:, :PK + HALF], e_all[h, :PK + HALF, :HALF]) * SCALE).astype(bf16).T
        dq_ref[HALF:, cols(h)] = (mm(kt[...], e_all[h, :, HALF:]) * SCALE).astype(bf16).T
        o_ref[:, cols(h)] = ot[h].astype(bf16).T

    def send_home(src, dst, i):
        c = pltpu.make_async_copy(src, dst, local.at[i])
        c.start()
        return c

    heads_loop(0, 2, last, 2)
    scatter.stage(3, 0)
    scatter.stage(1, 1)
    scatter.stage(0, 2)
    heads_loop(2, 4, last, 2)
    heads_loop(4, HEADS, last)
    scatter.stage(2, 1)
    scatter.stage(1, 2)
    scatter.stage(0, 3)
    drkv_ref[:, 0:D] = (dk[...] * SCALE).astype(bf16)
    drkv_ref[:, D:] = dv[...].astype(bf16)
    home = [send_home(drkv_ref, drkv_hbm, 2)]
    heads_loop(0, 4, rows_out)
    half = HEADS * D // 2
    home.append(send_home(o_ref.at[:, :half], o_hbm.at[:, :half], 3))
    home.append(send_home(dq_ref.at[:, :half], dq_hbm.at[:, :half], 4))
    scatter.stage(3, 1)
    scatter.stage(2, 2)
    scatter.stage(1, 3)
    heads_loop(4, HEADS, rows_out)
    home.append(send_home(o_ref.at[:, half:], o_hbm.at[:, half:], 5))
    home.append(send_home(dq_ref.at[:, half:], dq_hbm.at[:, half:], 6))
    scatter.stage(2, 3)
    scatter.stage(3, 2)
    scatter.stage(3, 3)
    for c in home:
        c.wait()
    go.drain()


def on_device(queries, resp_kv, prefix_kv, grad_out, held_block, resp_prompt, resp_len):
    bufs = []
    for n in range(8):
        for i in range(3):
            bufs.append(pltpu.VMEM((3,) + (SIDE,) * (2 - i) + (16, D), bf16))
    sm = pl.BlockSpec(memory_space=pltpu.SMEM)
    vm = pl.BlockSpec(memory_space=pltpu.VMEM)
    hbm = pl.BlockSpec(memory_space=pl.ANY)
    sems = 18 + 8 * 7 + 8 * 9 + 4
    outs = pl.pallas_call(
        kernel,
        out_shape=(jax.ShapeDtypeStruct(queries.shape, bf16), jax.ShapeDtypeStruct(queries.shape, bf16),
                   jax.ShapeDtypeStruct(resp_kv.shape, bf16), jax.ShapeDtypeStruct((64, 256), f32)),
        in_specs=[vm] + [sm] * 3 + [hbm] * 2 + [vm] * 2,
        out_specs=(hbm,) * 3 + (vm,),
        scratch_shapes=[pltpu.VMEM((2, SIDE, SIDE, SIDE, 16, D), bf16)] * 8
        + [pltpu.VMEM((SIDE, SIDE, k, 16, D), bf16) for k in (3, 3, 2)]
        + [pltpu.VMEM((BLOCKS, 32, D), bf16)] * 8 + [pltpu.VMEM((SIDE, SIDE, SIDE, 32, D), bf16)] * 4 + bufs
        + [pltpu.VMEM((ROWS, HEADS * D), bf16), pltpu.VMEM((ROWS, HEADS * D), bf16),
           pltpu.VMEM((NK, 2 * D), bf16), pltpu.VMEM((NK, 2 * D), bf16), pltpu.VMEM((D, NK), bf16),
           pltpu.VMEM((D, NK), bf16), pltpu.VMEM((HEADS, 2 * D, ROWS), bf16), pltpu.VMEM((HEADS, 2 * D, ROWS), bf16),
           pltpu.VMEM((HEADS, ROWS, D), bf16), pltpu.VMEM((HEADS, NK, ROWS), bf16),
           pltpu.SMEM((BLOCKS,), jnp.int32),
           pltpu.VMEM((CHUNKS + 1, HEADS, 1, ROWS), f32), pltpu.VMEM((HEADS, 1, ROWS), f32),
           pltpu.VMEM((HEADS, D, ROWS), f32), pltpu.VMEM((ROWS, HEADS * D), bf16), pltpu.VMEM((ROWS, HEADS * D), bf16),
           pltpu.VMEM((ROWS, 2 * D), bf16),
           pltpu.VMEM((ROWS, D), f32), pltpu.VMEM((ROWS, D), f32),
           pltpu.VMEM((CK, ROWS), f32), pltpu.VMEM((CK, ROWS), f32), pltpu.VMEM((CK, ROWS), bf16), pltpu.VMEM((CK, ROWS), bf16),
           pltpu.SemaphoreType.DMA((sems,)), pltpu.SemaphoreType.DMA((sems,)), pltpu.SemaphoreType.DMA((7,))],
        compiler_params=pltpu.CompilerParams(collective_id=0, has_side_effects=True, vmem_limit_bytes=62 * 2**20),
        name="shared",
    )(held_block, held_block, resp_prompt, resp_len, queries, grad_out, resp_kv, prefix_kv)
    return deliver(outs)


def deliver_kernel(*refs):
    n = len(refs) // 3
    sems = refs[-1]
    moves = []
    for i in range(n):
        src, dst, held = refs[i], refs[n + i], refs[2 * n + i]
        pieces = 4 if i < 2 else 1
        size = src.shape[0] // pieces
        for p in range(pieces):
            rows, k = slice(p * size, p * size + size), len(moves)
            moves.append((pltpu.make_async_copy(src.at[rows], held.at[rows], sems.at[0, k]),
                          pltpu.make_async_copy(held.at[rows], dst.at[rows], sems.at[1, k])))
    for bring, _ in moves:
        bring.start()
    for bring, leave in moves:
        bring.wait()
        leave.start()
    for _, leave in moves:
        leave.wait()


def deliver(arrays):
    hbm = pl.BlockSpec(memory_space=pl.ANY)
    return pl.pallas_call(
        deliver_kernel,
        out_shape=tuple(jax.ShapeDtypeStruct(a.shape, a.dtype) for a in arrays),
        in_specs=[hbm] * len(arrays),
        out_specs=(hbm,) * len(arrays),
        scratch_shapes=[pltpu.VMEM(a.shape, a.dtype) for a in arrays] + [pltpu.SemaphoreType.DMA((2, 10))],
        compiler_params=pltpu.CompilerParams(vmem_limit_bytes=62 * 2**20),
        name="deliver",
    )(*arrays)


def solution(mesh):
    rows = P("dp", None)
    return jax.shard_map(on_device, mesh=mesh, in_specs=(rows, rows, rows, rows, P(), P(), P()),
                         out_specs=(rows, rows, rows, rows), check_vma=False)
```

```python
import math

import jax
import jax.numpy as jnp
from jax import lax
from jax.experimental import pallas as pl
from jax.experimental.pallas import tpu as pltpu
from jax.sharding import PartitionSpec as P

f32, bf16 = jnp.float32, jnp.bfloat16
MESH = pl.DeviceIdType.MESH
NN = (((1,), (0,)), ((), ()))
SIDE = 4
D = 128
HEADS = 8
ROWS = 512
BLOCKS = 32
CHUNKS = 4
CK = 512
PK = CHUNKS * CK
NK = PK + ROWS
HALF = ROWS // 2
UNROLL = 4
SCALE = 1.0 / math.sqrt(D)
LOG2 = SCALE * math.log2(math.e)
ORDERS = ((0, 1, 2), (1, 2, 0), (2, 0, 1))
HOPS = (2, 1, 3)
PARTS = [(c, t) for c in range(CHUNKS) for t in range(2)]


def mm(a, b):
    return lax.dot_general(a, b, NN, preferred_element_type=f32)


def place():
    me = lax.axis_index("dp")
    return (me // 32, me // 8 % SIDE, me // 2 % SIDE), me % 2


def device(at, core):
    return ((at[0] * SIDE + at[1]) * SIDE + at[2]) * 2 + core


def moved(at, axis, step):
    return tuple((c + step) % SIDE if a == axis else c for a, c in enumerate(at))


class Sender:
    def __init__(self, send, recv):
        self.send, self.recv, self.count, self.all = send, recv, 0, []

    def __call__(self, src, dst, to):
        c = self.ready(src, dst, to)
        c.start()
        return c

    def ready(self, src, dst, to):
        i = self.count
        self.count += 1
        c = pltpu.make_async_remote_copy(src_ref=src, dst_ref=dst, send_sem=self.send.at[i], recv_sem=self.recv.at[i],
                                         device_id=(to,), device_id_type=MESH)
        self.all.append(c)
        return c

    def drain(self):
        for c in self.all:
            c.wait_send()


class Gather:
    def __init__(self, go, at, core, refs, stages):
        self.go, self.at, self.core, self.refs, self.stages = go, at, core, refs, stages
        self.flying = {}

    def put(self, x_ref):
        for n, (c, t) in enumerate(PARTS):
            a, b, _ = ORDERS[n % 3]
            self.stages[n % 3][n // 3, self.at[b], self.at[a]] = x_ref[16 * c:16 * c + 16, D * t:D * t + D]

    def start(self, k, i):
        a, b, _ = ORDERS[k]
        v = self.stages[k].at[:, self.at[b], self.at[a]] if i == 0 else self.stages[k].at[:, self.at[b]]
        self.flying[k, i] = [self.go(v, v, device(moved(self.at, ORDERS[k][i], s), self.core)) for s in HOPS]

    def start_last(self, n):
        a = ORDERS[n % 3][2]
        src, dst = self.stages[n % 3].at[n // 3], self.refs[n].at[self.core, self.at[a]]
        self.flying["part", n] = [self.go(src, dst, device(moved(self.at, a, s), self.core)) for s in HOPS]
        self.refs[n][self.core, self.at[a]] = self.stages[n % 3][n // 3]

    def wait(self, *key):
        for c in self.flying[key]:
            c.wait_recv()

    def pass_on(self, n):
        p, to = self.at[ORDERS[n % 3][2]], device(self.at, 1 - self.core)
        self.flying["core", n] = []
        for near in (None, 1, 2, 0):
            k = p
            if near is not None:
                self.flying["part", n][near].wait_recv()
                k = (p + SIDE - HOPS[near]) % SIDE
            v = self.refs[n].at[self.core, k]
            self.flying["core", n].append(self.go(v, v, to))


class Scatter:
    def __init__(self, go, at, core, held, prompt, own, peer, w, bufs, out):
        self.go, self.at, self.core, self.held, self.prompt = go, at, core, held, prompt
        self.own, self.peer, self.w, self.bufs, self.out = own, peer, w, bufs, out
        self.flying = {}
        self.coord = [[(at[a] + s) % SIDE for s in HOPS] for a in range(3)]
        self.dev = [[device(moved(at, a, s), core) for s in HOPS] for a in range(3)]
        self.other_core = device(at, 1 - core)

    def swap(self, c):
        self.flying[c] = self.go(self.own[c].at[0:BLOCKS], self.peer[c].at[0:BLOCKS], self.other_core)

    def fill(self, c):
        self.flying[c].wait_recv()
        mine = self.prompt[device(self.at, self.core)]
        other = self.prompt[device(self.at, 1 - self.core)]
        own, peer = self.own[c], self.peer[c]

        def body(j, _):
            for u in range(8):
                b = self.held[(j * 8 + u) * 2 + self.core]
                p, k = lax.shift_right_logical(b, 5), lax.bitwise_and(b, 31)
                v = own[jnp.where(p == mine, k, BLOCKS)] + peer[jnp.where(p == other, k, BLOCKS)]
                to = (j // 2, j % 2 * 2 + u // 4, u % 4)
                for t in range(2):
                    n = 2 * c + t
                    self.w[n][tuple(to[a] for a in ORDERS[n % 3])] = v[16 * t:16 * t + 16]
            return 0

        lax.fori_loop(0, 8, body, 0)

    def spot(self, n, i, k):
        return tuple(self.at[a] for a in ORDERS[n % 3][:i]) + (k,)

    def ready(self, c, i):
        for n in (2 * c, 2 * c + 1):
            a = ORDERS[n % 3][i]
            self.flying[n, i] = [
                self.go.ready(self.w[n].at[self.spot(n, i, self.coord[a][j])], self.bufs[3 * n + i].at[j], self.dev[a][j])
                for j in range(3)]

    def start(self, c, i):
        if (2 * c, i) not in self.flying:
            self.ready(c, i)
        for n in (2 * c, 2 * c + 1):
            for f in self.flying[n, i]:
                f.start()

    def add(self, c, i):
        for n in (2 * c, 2 * c + 1):
            for f in self.flying[n, i]:
                f.wait_recv()
            buf = self.bufs[3 * n + i]
            here = self.spot(n, i, self.at[ORDERS[n % 3][i]])
            total = (self.w[n][here].astype(f32) + buf[0].astype(f32)) + (buf[1].astype(f32) + buf[2].astype(f32))
            if i < 2:
                self.w[n][here] = total.astype(bf16)
            else:
                t = n % 2
                self.out[16 * c:16 * c + 16, D * t:D * t + D] = total

    def stage(self, c, s):
        if s == 0:
            self.fill(c)
            self.start(c, 0)
        else:
            self.add(c, s - 1)
            if s < 3:
                self.start(c, s)


def kernel(held_vec, held_ref, prompt_ref, len_ref, q_hbm, g_hbm, rkv_ref, x_ref, o_hbm, dq_hbm, drkv_hbm, out_ref, *rest):
    gref, stages, rest = rest[:8], rest[8:11], rest[11:]
    own, peer, w, bufs, rest = rest[:4], rest[4:8], rest[8:16], rest[16:40], rest[40:]
    q_ref, g_ref, kk, vv, kt, vt, q2t, g2t, gp, e_all, loc_ref, ms, ls, ot, o_ref, dq_ref, drkv_ref, dk, dv, s0, s1, p0, p1, send, recv, local = rest
    at, core = place()
    me = device(at, core)
    barrier = pltpu.get_barrier_semaphore()
    near = [device(moved(at, a, s), core) for a in range(3) for s in HOPS] + [device(at, 1 - core)]
    for n in near:
        pl.semaphore_signal(barrier, inc=1, device_id=(n,), device_id_type=MESH)
    q_in = pltpu.make_async_copy(q_hbm, q_ref, local.at[0])
    g_in = pltpu.make_async_copy(g_hbm, g_ref, local.at[1])
    q_in.start()
    g_in.start()
    go = Sender(send, recv)
    gather = Gather(go, at, core, gref, stages)
    gather.put(x_ref)
    pl.semaphore_wait(barrier, len(near))
    for k in range(3):
        gather.start(k, 0)

    for ref in (*own, *peer):
        ref[BLOCKS] = jnp.zeros((32, D), bf16)
    length = len_ref[me]
    live = lax.broadcasted_iota(jnp.int32, (1, ROWS), 1) < length
    tri = lax.broadcasted_iota(jnp.int32, (HALF, HALF), 0) <= lax.broadcasted_iota(jnp.int32, (HALF, HALF), 1)
    vv[:, D:] = jnp.ones((NK, D), bf16)

    def heads_loop(lo, hi, item, step=UNROLL):
        def body(i, _):
            for u in range(step):
                item(i * step + u)
            return 0
        lax.fori_loop(lo // step, hi // step, body, 0)

    def staged(ahead, item, slots):
        slots[0][...] = ahead(0)

        def body(i, _):
            for u in range(UNROLL):
                h = i * UNROLL + u
                slots[(u + 1) % 2][...] = ahead(lax.rem(h + 1, HEADS))
                item(h, slots[u % 2])
            return 0
        lax.fori_loop(0, HEADS // UNROLL, body, 0)

    def straight(ahead, item, slots, middle):
        slots[0][...] = ahead(0)
        for h in range(HEADS):
            if h == HEADS // 2:
                for job in middle:
                    scatter.stage(*job)
            if h + 1 < HEADS:
                slots[(h + 1) % 2][...] = ahead(h + 1)
            item(h, slots[h % 2])

    def cols(h):
        if isinstance(h, int):
            return slice(h * D, h * D + D)
        return pl.ds(pl.multiple_of(h * D, D), D)

    def prepare(h):
        qs = q_ref[:, cols(h)].astype(f32) * LOG2
        hi = qs.astype(bf16)
        lo = (qs - hi.astype(f32)).astype(bf16)
        q2t[h, 0:D] = hi.T
        q2t[h, D:] = lo.T
        g2t[h, 0:D] = g_ref[:, cols(h)].T
        g2t[h, D + 16:] = jnp.zeros((D - 16, ROWS), bf16)

    def place_keys(k0, kn, keys, vals):
        kk[k0:k0 + kn, 0:D] = keys
        kk[k0:k0 + kn, D:] = keys
        vv[k0:k0 + kn, 0:D] = vals

    def turn(k0, kn):
        kt[:, k0:k0 + kn] = kk[k0:k0 + kn, 0:D].T
        vt[:, k0:k0 + kn] = vv[k0:k0 + kn, 0:D].T

    def first(h):
        sa = mm(kk[PK:PK + HALF, :], q2t[h])
        sa = jnp.concatenate([jnp.where(tri, sa[:, :HALF], -1e30), sa[:, HALF:]], axis=1)
        sb = jnp.where(tri, mm(kk[PK + HALF:, :], q2t[h, :, HALF:]), -1e30)
        m = jnp.max(sa, axis=0, keepdims=True)
        m = jnp.concatenate([m[:, :HALF], jnp.maximum(m[:, HALF:], jnp.max(sb, axis=0, keepdims=True))], axis=1)
        ea = jnp.exp2(sa - m)
        eb = jnp.exp2(sb - m[:, HALF:])
        l = jnp.sum(ea, axis=0, keepdims=True)
        l = jnp.concatenate([l[:, :HALF], l[:, HALF:] + jnp.sum(eb, axis=0, keepdims=True)], axis=1)
        ea, eb = ea.astype(bf16), eb.astype(bf16)
        e_all[h, PK:PK + HALF, :] = ea
        e_all[h, PK + HALF:, HALF:] = eb
        oa = mm(vt[:, PK:PK + HALF], ea)
        ob = mm(vt[:, PK + HALF:], eb)
        ms[0, h] = m
        ls[h] = l
        ot[h, :, 0:HALF] = oa[:, :HALF]
        ot[h, :, HALF:] = oa[:, HALF:] + ob

    def forward(c):
        k0 = c * CK

        def ahead(h):
            return mm(kk[k0:k0 + CK, :], q2t[h])

        def item(h, s):
            old = ms[c, h]
            m = jnp.maximum(old, jnp.max(s[...], axis=0, keepdims=True))
            e = jnp.exp2(s[...] - m)
            fade = jnp.exp2(old - m)
            ls[h] = ls[h] * fade + jnp.sum(e, axis=0, keepdims=True)
            e = e.astype(bf16)
            e_all[h, k0:k0 + CK, :] = e
            ot[h] = ot[h] * fade + mm(vt[:, k0:k0 + CK], e)
            ms[c + 1, h] = m
        staged(ahead, item, (s0, s1))

    def finish(h):
        f = jnp.where(live, 1.0 / ls[h], 0.0)
        o = ot[h] * f
        ot[h] = o
        gt = g2t[h, 0:D].astype(f32)
        gt = jnp.where(live, gt, 0.0) * f
        neg = -jnp.sum(gt * o, axis=0, keepdims=True)
        gb = gt.astype(bf16)
        gp[h] = gb.T
        hi = neg.astype(bf16).astype(f32)
        sub = lax.broadcasted_iota(jnp.int32, (16, ROWS), 0)
        extra = jnp.where(sub == 0, hi, jnp.where(sub == 1, neg - hi, 0.0)).astype(bf16)
        g2t[h, 0:D] = gb
        g2t[h, D:D + 16] = extra

    def slope(h, k0, kn, r0):
        return mm(vv[k0:k0 + kn, :], g2t[h, :, r0:]).astype(bf16)

    def back(h, dp, k0, kn, r0, stage, a0):
        fade = jnp.exp2(ms[stage, h] - ms[CHUNKS, h]).astype(bf16)[:, r0:]
        e = e_all[h, k0:k0 + kn, r0:] * fade
        ds = e * dp
        e_all[h, k0:k0 + kn, r0:] = ds
        dk[a0:a0 + kn, :] += mm(ds, q_ref[r0:, cols(h)])
        dv[a0:a0 + kn, :] += mm(e, gp[h, r0:, :])

    def load_chunk(c):
        for n in (2 * c, 2 * c + 1):
            gather.wait("core", n)
        for b in range(BLOCKS):
            n = loc_ref[b]
            held_at = (lax.shift_right_logical(n, 5), lax.bitwise_and(lax.shift_right_logical(n, 3), 3),
                       lax.bitwise_and(lax.shift_right_logical(n, 1), 3))
            keys, vals = [gref[p][(lax.bitwise_and(n, 1),) + tuple(held_at[ORDERS[p % 3][i]] for i in (2, 1, 0))]
                          for p in (2 * c, 2 * c + 1)]
            place_keys(c * CK + 16 * b, 16, keys, vals)
        turn(c * CK, CK)

    place_keys(PK, ROWS, rkv_ref[:, 0:D], rkv_ref[:, D:])
    turn(PK, ROWS)
    q_in.wait()
    g_in.wait()
    heads_loop(0, HEADS, prepare)
    for k in range(3):
        gather.wait(k, 0)
        gather.start(k, 1)
    heads_loop(0, 4, first)
    for k in range(3):
        gather.wait(k, 1)
    for n in range(8):
        gather.start_last(n)
    heads_loop(4, HEADS, first)

    lane = lax.broadcasted_iota(jnp.int32, (1, 128), 1)
    held_row = held_vec[...].reshape(1, 128)
    base = prompt_ref[me] * BLOCKS
    for b in range(BLOCKS):
        loc_ref[b] = jnp.max(jnp.where(held_row == base + b, lane, 0))

    def pass_on(c):
        for n in (2 * c, 2 * c + 1):
            gather.pass_on(n)

    pass_on(0)
    for c in range(CHUNKS):
        load_chunk(c)
        if c + 1 < CHUNKS:
            pass_on(c + 1)
        forward(c)
    heads_loop(0, HEADS, finish)

    scatter = Scatter(go, at, core, held_ref, prompt_ref, own, peer, w, bufs, out_ref)
    for c in range(CHUNKS):
        dk[...] = jnp.zeros_like(dk)
        dv[...] = jnp.zeros_like(dv)
        middle = [] if c == 0 else [(c - 1, 0)] if c < 3 else [(2, 0), (0, 1)]
        straight(lambda h: slope(h, c * CK, CK, 0), lambda h, dp: back(h, dp[...], c * CK, CK, 0, c + 1, 0), (p0, p1), middle)
        own[c][0:BLOCKS, 0:16, :] = (dk[...] * SCALE).astype(bf16).reshape(BLOCKS, 16, D)
        own[c][0:BLOCKS, 16:, :] = dv[...].astype(bf16).reshape(BLOCKS, 16, D)
        scatter.swap(c)
    dk[...] = jnp.zeros_like(dk)
    dv[...] = jnp.zeros_like(dv)

    def last(h):
        back(h, slope(h, PK, HALF, 0), PK, HALF, 0, 0, 0)
        back(h, slope(h, PK + HALF, HALF, HALF), PK + HALF, HALF, HALF, 0, HALF)

    def rows_out(h):
        dq_ref[:HALF, cols(h)] = (mm(kt[:, :PK + HALF], e_all[h, :PK + HALF, :HALF]) * SCALE).astype(bf16).T
        dq_ref[HALF:, cols(h)] = (mm(kt[...], e_all[h, :, HALF:]) * SCALE).astype(bf16).T
        o_ref[:, cols(h)] = ot[h].astype(bf16).T

    def send_home(src, dst, i):
        c = pltpu.make_async_copy(src, dst, local.at[i])
        c.start()
        return c

    heads_loop(0, 2, last, 2)
    scatter.stage(3, 0)
    scatter.stage(1, 1)
    scatter.stage(0, 2)
    heads_loop(2, 4, last, 2)
    heads_loop(4, HEADS, last)
    scatter.stage(2, 1)
    scatter.stage(1, 2)
    scatter.stage(0, 3)
    drkv_ref[:, 0:D] = (dk[...] * SCALE).astype(bf16)
    drkv_ref[:, D:] = dv[...].astype(bf16)
    home = [send_home(drkv_ref, drkv_hbm, 2)]
    heads_loop(0, 4, rows_out)
    half = HEADS * D // 2
    home.append(send_home(o_ref.at[:, :half], o_hbm.at[:, :half], 3))
    home.append(send_home(dq_ref.at[:, :half], dq_hbm.at[:, :half], 4))
    scatter.stage(3, 1)
    scatter.stage(2, 2)
    scatter.stage(1, 3)
    heads_loop(4, HEADS, rows_out)
    home.append(send_home(o_ref.at[:, half:], o_hbm.at[:, half:], 5))
    home.append(send_home(dq_ref.at[:, half:], dq_hbm.at[:, half:], 6))
    scatter.stage(2, 3)
    scatter.stage(3, 2)
    scatter.stage(3, 3)
    for c in home:
        c.wait()
    go.drain()


def on_device(queries, resp_kv, prefix_kv, grad_out, held_block, resp_prompt, resp_len):
    bufs = []
    for n in range(8):
        for i in range(3):
            bufs.append(pltpu.VMEM((3,) + (SIDE,) * (2 - i) + (16, D), bf16))
    sm = pl.BlockSpec(memory_space=pltpu.SMEM)
    vm = pl.BlockSpec(memory_space=pltpu.VMEM)
    hbm = pl.BlockSpec(memory_space=pl.ANY)
    sems = 18 + 8 * 7 + 8 * 9 + 4
    outs = pl.pallas_call(
        kernel,
        out_shape=(jax.ShapeDtypeStruct(queries.shape, bf16), jax.ShapeDtypeStruct(queries.shape, bf16),
                   jax.ShapeDtypeStruct(resp_kv.shape, bf16), jax.ShapeDtypeStruct((64, 256), f32)),
        in_specs=[vm] + [sm] * 3 + [hbm] * 2 + [vm] * 2,
        out_specs=(hbm,) * 3 + (vm,),
        scratch_shapes=[pltpu.VMEM((2, SIDE, SIDE, SIDE, 16, D), bf16)] * 8
        + [pltpu.VMEM((k, SIDE, SIDE, 16, D), bf16) for k in (3, 3, 2)]
        + [pltpu.VMEM((BLOCKS + 1, 32, D), bf16)] * 8 + [pltpu.VMEM((SIDE, SIDE, SIDE, 16, D), bf16)] * 8 + bufs
        + [pltpu.VMEM((ROWS, HEADS * D), bf16), pltpu.VMEM((ROWS, HEADS * D), bf16),
           pltpu.VMEM((NK, 2 * D), bf16), pltpu.VMEM((NK, 2 * D), bf16), pltpu.VMEM((D, NK), bf16),
           pltpu.VMEM((D, NK), bf16), pltpu.VMEM((HEADS, 2 * D, ROWS), bf16), pltpu.VMEM((HEADS, 2 * D, ROWS), bf16),
           pltpu.VMEM((HEADS, ROWS, D), bf16), pltpu.VMEM((HEADS, NK, ROWS), bf16),
           pltpu.SMEM((BLOCKS,), jnp.int32),
           pltpu.VMEM((CHUNKS + 1, HEADS, 1, ROWS), f32), pltpu.VMEM((HEADS, 1, ROWS), f32),
           pltpu.VMEM((HEADS, D, ROWS), f32), pltpu.VMEM((ROWS, HEADS * D), bf16), pltpu.VMEM((ROWS, HEADS * D), bf16),
           pltpu.VMEM((ROWS, 2 * D), bf16),
           pltpu.VMEM((ROWS, D), f32), pltpu.VMEM((ROWS, D), f32),
           pltpu.VMEM((CK, ROWS), f32), pltpu.VMEM((CK, ROWS), f32), pltpu.VMEM((CK, ROWS), bf16), pltpu.VMEM((CK, ROWS), bf16),
           pltpu.SemaphoreType.DMA((sems,)), pltpu.SemaphoreType.DMA((sems,)), pltpu.SemaphoreType.DMA((7,))],
        compiler_params=pltpu.CompilerParams(collective_id=0, has_side_effects=True, vmem_limit_bytes=62 * 2**20),
        name="shared",
    )(held_block, held_block, resp_prompt, resp_len, queries, grad_out, resp_kv, prefix_kv)
    return deliver(outs)


def deliver_kernel(*refs):
    n = len(refs) // 3
    sems = refs[-1]
    moves = []
    for i in range(n):
        src, dst, held = refs[i], refs[n + i], refs[2 * n + i]
        pieces = 4 if i < 2 else 1
        size = src.shape[0] // pieces
        for p in range(pieces):
            rows, k = slice(p * size, p * size + size), len(moves)
            moves.append((pltpu.make_async_copy(src.at[rows], held.at[rows], sems.at[0, k]),
                          pltpu.make_async_copy(held.at[rows], dst.at[rows], sems.at[1, k])))
    for bring, _ in moves:
        bring.start()
    for bring, leave in moves:
        bring.wait()
        leave.start()
    for _, leave in moves:
        leave.wait()


def deliver(arrays):
    hbm = pl.BlockSpec(memory_space=pl.ANY)
    return pl.pallas_call(
        deliver_kernel,
        out_shape=tuple(jax.ShapeDtypeStruct(a.shape, a.dtype) for a in arrays),
        in_specs=[hbm] * len(arrays),
        out_specs=(hbm,) * len(arrays),
        scratch_shapes=[pltpu.VMEM(a.shape, a.dtype) for a in arrays] + [pltpu.SemaphoreType.DMA((2, 10))],
        compiler_params=pltpu.CompilerParams(vmem_limit_bytes=62 * 2**20),
        name="deliver",
    )(*arrays)


def solution(mesh):
    rows = P("dp", None)
    return jax.shard_map(on_device, mesh=mesh, in_specs=(rows, rows, rows, rows, P(), P(), P()),
                         out_specs=(rows, rows, rows, rows), check_vma=False)
```

```python
import math

import jax
import jax.numpy as jnp
from jax import lax
from jax.experimental import pallas as pl
from jax.experimental.pallas import tpu as pltpu
from jax.sharding import PartitionSpec as P

f32, bf16 = jnp.float32, jnp.bfloat16
MESH = pl.DeviceIdType.MESH
NN = (((1,), (0,)), ((), ()))
SIDE = 4
D = 128
HEADS = 8
ROWS = 512
BLOCKS = 32
CHUNKS = 4
CK = 512
PK = CHUNKS * CK
NK = PK + ROWS
HALF = ROWS // 2
UNROLL = 4
SCALE = 1.0 / math.sqrt(D)
LOG2 = SCALE * math.log2(math.e)
ORDERS = ((0, 1, 2), (1, 2, 0), (2, 0, 1))
HOPS = (2, 1, 3)
PARTS = [(c, t) for c in range(CHUNKS) for t in range(2)]


def mm(a, b):
    return lax.dot_general(a, b, NN, preferred_element_type=f32)


def place():
    me = lax.axis_index("dp")
    return (me // 32, me // 8 % SIDE, me // 2 % SIDE), me % 2


def device(at, core):
    return ((at[0] * SIDE + at[1]) * SIDE + at[2]) * 2 + core


def moved(at, axis, step):
    return tuple((c + step) % SIDE if a == axis else c for a, c in enumerate(at))


class Sender:
    def __init__(self, send, recv):
        self.send, self.recv, self.count, self.all = send, recv, 0, []

    def __call__(self, src, dst, to):
        c = self.ready(src, dst, to)
        c.start()
        return c

    def ready(self, src, dst, to):
        i = self.count
        self.count += 1
        c = pltpu.make_async_remote_copy(src_ref=src, dst_ref=dst, send_sem=self.send.at[i], recv_sem=self.recv.at[i],
                                         device_id=(to,), device_id_type=MESH)
        self.all.append(c)
        return c

    def drain(self):
        for c in self.all:
            c.wait_send()


class Gather:
    def __init__(self, go, at, core, refs, stages):
        self.go, self.at, self.core, self.refs, self.stages = go, at, core, refs, stages
        self.flying = {}

    def put(self, x_ref):
        for n, (c, t) in enumerate(PARTS):
            a, b, _ = ORDERS[n % 3]
            self.stages[n % 3][n // 3, self.at[b], self.at[a]] = x_ref[16 * c:16 * c + 16, D * t:D * t + D]

    def start(self, k, i):
        a, b, _ = ORDERS[k]
        v = self.stages[k].at[:, self.at[b], self.at[a]] if i == 0 else self.stages[k].at[:, self.at[b]]
        self.flying[k, i] = [self.go(v, v, device(moved(self.at, ORDERS[k][i], s), self.core)) for s in HOPS]

    def start_last(self, n):
        a = ORDERS[n % 3][2]
        src, dst = self.stages[n % 3].at[n // 3], self.refs[n].at[self.core, self.at[a]]
        self.flying["part", n] = [self.go(src, dst, device(moved(self.at, a, s), self.core)) for s in HOPS]
        self.refs[n][self.core, self.at[a]] = self.stages[n % 3][n // 3]

    def wait(self, *key):
        for c in self.flying[key]:
            c.wait_recv()

    def pass_on(self, n):
        p, to = self.at[ORDERS[n % 3][2]], device(self.at, 1 - self.core)
        self.flying["core", n] = []
        for near in (None, 1, 2, 0):
            k = p
            if near is not None:
                self.flying["part", n][near].wait_recv()
                k = (p + SIDE - HOPS[near]) % SIDE
            v = self.refs[n].at[self.core, k]
            self.flying["core", n].append(self.go(v, v, to))


class Scatter:
    def __init__(self, go, at, core, held, prompt, own, peer, w, bufs, out):
        self.go, self.at, self.core, self.held, self.prompt = go, at, core, held, prompt
        self.own, self.peer, self.w, self.bufs, self.out = own, peer, w, bufs, out
        self.flying = {}
        self.coord = [[(at[a] + s) % SIDE for s in HOPS] for a in range(3)]
        self.dev = [[device(moved(at, a, s), core) for s in HOPS] for a in range(3)]
        self.other_core = device(at, 1 - core)

    def swap(self, c):
        self.flying[c] = self.go(self.own[c].at[0:BLOCKS], self.peer[c].at[0:BLOCKS], self.other_core)

    def fill(self, c):
        self.flying[c].wait_recv()
        mine = self.prompt[device(self.at, self.core)]
        other = self.prompt[device(self.at, 1 - self.core)]
        own, peer = self.own[c], self.peer[c]

        def body(j, _):
            for u in range(8):
                b = self.held[(j * 8 + u) * 2 + self.core]
                p, k = lax.shift_right_logical(b, 5), lax.bitwise_and(b, 31)
                v = own[jnp.where(p == mine, k, BLOCKS)] + peer[jnp.where(p == other, k, BLOCKS)]
                to = (j // 2, j % 2 * 2 + u // 4, u % 4)
                for t in range(2):
                    n = 2 * c + t
                    self.w[n][tuple(to[a] for a in ORDERS[n % 3])] = v[16 * t:16 * t + 16]
            return 0

        lax.fori_loop(0, 8, body, 0)

    def spot(self, n, i, k):
        return tuple(self.at[a] for a in ORDERS[n % 3][:i]) + (k,)

    def ready(self, c, i):
        for n in (2 * c, 2 * c + 1):
            a = ORDERS[n % 3][i]
            self.flying[n, i] = [
                self.go.ready(self.w[n].at[self.spot(n, i, self.coord[a][j])], self.bufs[3 * n + i].at[j], self.dev[a][j])
                for j in range(3)]

    def start(self, c, i):
        if (2 * c, i) not in self.flying:
            self.ready(c, i)
        for n in (2 * c, 2 * c + 1):
            for f in self.flying[n, i]:
                f.start()

    def add(self, c, i):
        for n in (2 * c, 2 * c + 1):
            for f in self.flying[n, i]:
                f.wait_recv()
            buf = self.bufs[3 * n + i]
            here = self.spot(n, i, self.at[ORDERS[n % 3][i]])
            total = (self.w[n][here].astype(f32) + buf[0].astype(f32)) + (buf[1].astype(f32) + buf[2].astype(f32))
            if i < 2:
                self.w[n][here] = total.astype(bf16)
            else:
                t = n % 2
                self.out[16 * c:16 * c + 16, D * t:D * t + D] = total

    def stage(self, c, s):
        if s == 0:
            self.fill(c)
            self.start(c, 0)
        else:
            self.add(c, s - 1)
            if s < 3:
                self.start(c, s)


def kernel(held_vec, held_ref, prompt_ref, len_ref, q_hbm, g_hbm, rkv_ref, x_ref, o_hbm, dq_hbm, drkv_hbm, out_ref, *rest):
    gref, stages, rest = rest[:8], rest[8:11], rest[11:]
    own, peer, w, bufs, rest = rest[:4], rest[4:8], rest[8:16], rest[16:40], rest[40:]
    q_ref, g_ref, kk, vv, kt, vt, q2t, g2t, gp, e_all, loc_ref, ms, ls, ot, o_ref, dq_ref, drkv_ref, dk, dv, s0, s1, p0, p1, send, recv, local = rest
    at, core = place()
    me = device(at, core)
    barrier = pltpu.get_barrier_semaphore()
    near = [device(moved(at, a, s), core) for a in range(3) for s in HOPS] + [device(at, 1 - core)]
    for n in near:
        pl.semaphore_signal(barrier, inc=1, device_id=(n,), device_id_type=MESH)
    q_in = pltpu.make_async_copy(q_hbm, q_ref, local.at[0])
    g_in = pltpu.make_async_copy(g_hbm, g_ref, local.at[1])
    q_in.start()
    g_in.start()
    go = Sender(send, recv)
    gather = Gather(go, at, core, gref, stages)
    gather.put(x_ref)
    pl.semaphore_wait(barrier, len(near))
    for k in range(3):
        gather.start(k, 0)

    for ref in (*own, *peer):
        ref[BLOCKS] = jnp.zeros((32, D), bf16)
    length = len_ref[me]
    live = lax.broadcasted_iota(jnp.int32, (1, ROWS), 1) < length
    tri = lax.broadcasted_iota(jnp.int32, (HALF, HALF), 0) <= lax.broadcasted_iota(jnp.int32, (HALF, HALF), 1)
    vv[:, D:] = jnp.ones((NK, D), bf16)

    def heads_loop(lo, hi, item, step=UNROLL):
        def body(i, _):
            for u in range(step):
                item(i * step + u)
            return 0
        lax.fori_loop(lo // step, hi // step, body, 0)

    def staged(ahead, item, slots, middle=()):
        slots[0][...] = ahead(0)

        for job in middle:
            scatter.ready(*job)

        def between():
            for job in middle:
                scatter.stage(*job)

        def body(i, _):
            if middle:
                pl.when(i == 1)(between)
            for u in range(UNROLL):
                h = i * UNROLL + u
                slots[(u + 1) % 2][...] = ahead(lax.rem(h + 1, HEADS))
                item(h, slots[u % 2])
            return 0
        lax.fori_loop(0, HEADS // UNROLL, body, 0)

    def cols(h):
        if isinstance(h, int):
            return slice(h * D, h * D + D)
        return pl.ds(pl.multiple_of(h * D, D), D)

    def prepare(h):
        qs = q_ref[:, cols(h)].astype(f32) * LOG2
        hi = qs.astype(bf16)
        lo = (qs - hi.astype(f32)).astype(bf16)
        q2t[h, 0:D] = hi.T
        q2t[h, D:] = lo.T
        g2t[h, 0:D] = g_ref[:, cols(h)].T
        g2t[h, D + 16:] = jnp.zeros((D - 16, ROWS), bf16)

    def place_keys(k0, kn, keys, vals):
        kk[k0:k0 + kn, 0:D] = keys
        kk[k0:k0 + kn, D:] = keys
        vv[k0:k0 + kn, 0:D] = vals

    def turn(k0, kn):
        kt[:, k0:k0 + kn] = kk[k0:k0 + kn, 0:D].T
        vt[:, k0:k0 + kn] = vv[k0:k0 + kn, 0:D].T

    def first(h):
        sa = mm(kk[PK:PK + HALF, :], q2t[h])
        sa = jnp.concatenate([jnp.where(tri, sa[:, :HALF], -1e30), sa[:, HALF:]], axis=1)
        sb = jnp.where(tri, mm(kk[PK + HALF:, :], q2t[h, :, HALF:]), -1e30)
        m = jnp.max(sa, axis=0, keepdims=True)
        m = jnp.concatenate([m[:, :HALF], jnp.maximum(m[:, HALF:], jnp.max(sb, axis=0, keepdims=True))], axis=1)
        ea = jnp.exp2(sa - m)
        eb = jnp.exp2(sb - m[:, HALF:])
        l = jnp.sum(ea, axis=0, keepdims=True)
        l = jnp.concatenate([l[:, :HALF], l[:, HALF:] + jnp.sum(eb, axis=0, keepdims=True)], axis=1)
        ea, eb = ea.astype(bf16), eb.astype(bf16)
        e_all[h, PK:PK + HALF, :] = ea
        e_all[h, PK + HALF:, HALF:] = eb
        oa = mm(vt[:, PK:PK + HALF], ea)
        ob = mm(vt[:, PK + HALF:], eb)
        ms[0, h] = m
        ls[h] = l
        ot[h, :, 0:HALF] = oa[:, :HALF]
        ot[h, :, HALF:] = oa[:, HALF:] + ob

    def forward(c):
        k0 = c * CK

        def ahead(h):
            return mm(kk[k0:k0 + CK, :], q2t[h])

        def item(h, s):
            old = ms[c, h]
            m = jnp.maximum(old, jnp.max(s[...], axis=0, keepdims=True))
            e = jnp.exp2(s[...] - m)
            fade = jnp.exp2(old - m)
            ls[h] = ls[h] * fade + jnp.sum(e, axis=0, keepdims=True)
            e = e.astype(bf16)
            e_all[h, k0:k0 + CK, :] = e
            ot[h] = ot[h] * fade + mm(vt[:, k0:k0 + CK], e)
            ms[c + 1, h] = m
        staged(ahead, item, (s0, s1))

    def finish(h):
        f = jnp.where(live, 1.0 / ls[h], 0.0)
        o = ot[h] * f
        ot[h] = o
        gt = g2t[h, 0:D].astype(f32)
        gt = jnp.where(live, gt, 0.0) * f
        neg = -jnp.sum(gt * o, axis=0, keepdims=True)
        gb = gt.astype(bf16)
        gp[h] = gb.T
        hi = neg.astype(bf16).astype(f32)
        sub = lax.broadcasted_iota(jnp.int32, (16, ROWS), 0)
        extra = jnp.where(sub == 0, hi, jnp.where(sub == 1, neg - hi, 0.0)).astype(bf16)
        g2t[h, 0:D] = gb
        g2t[h, D:D + 16] = extra

    def slope(h, k0, kn, r0):
        return mm(vv[k0:k0 + kn, :], g2t[h, :, r0:]).astype(bf16)

    def back(h, dp, k0, kn, r0, stage, a0):
        fade = jnp.exp2(ms[stage, h] - ms[CHUNKS, h]).astype(bf16)[:, r0:]
        e = e_all[h, k0:k0 + kn, r0:] * fade
        ds = e * dp
        e_all[h, k0:k0 + kn, r0:] = ds
        dk[a0:a0 + kn, :] += mm(ds, q_ref[r0:, cols(h)])
        dv[a0:a0 + kn, :] += mm(e, gp[h, r0:, :])

    def load_chunk(c):
        for n in (2 * c, 2 * c + 1):
            gather.wait("core", n)
        for b in range(BLOCKS):
            n = loc_ref[b]
            held_at = (lax.shift_right_logical(n, 5), lax.bitwise_and(lax.shift_right_logical(n, 3), 3),
                       lax.bitwise_and(lax.shift_right_logical(n, 1), 3))
            keys, vals = [gref[p][(lax.bitwise_and(n, 1),) + tuple(held_at[ORDERS[p % 3][i]] for i in (2, 1, 0))]
                          for p in (2 * c, 2 * c + 1)]
            place_keys(c * CK + 16 * b, 16, keys, vals)
        turn(c * CK, CK)

    place_keys(PK, ROWS, rkv_ref[:, 0:D], rkv_ref[:, D:])
    turn(PK, ROWS)
    q_in.wait()
    g_in.wait()
    heads_loop(0, HEADS, prepare)
    for k in range(3):
        gather.wait(k, 0)
        gather.start(k, 1)
    heads_loop(0, 4, first)
    for k in range(3):
        gather.wait(k, 1)
    for n in range(8):
        gather.start_last(n)
    heads_loop(4, HEADS, first)

    lane = lax.broadcasted_iota(jnp.int32, (1, 128), 1)
    held_row = held_vec[...].reshape(1, 128)
    base = prompt_ref[me] * BLOCKS
    for b in range(BLOCKS):
        loc_ref[b] = jnp.max(jnp.where(held_row == base + b, lane, 0))

    def pass_on(c):
        for n in (2 * c, 2 * c + 1):
            gather.pass_on(n)

    pass_on(0)
    for c in range(CHUNKS):
        load_chunk(c)
        if c + 1 < CHUNKS:
            pass_on(c + 1)
        forward(c)
    heads_loop(0, HEADS, finish)

    scatter = Scatter(go, at, core, held_ref, prompt_ref, own, peer, w, bufs, out_ref)
    for c in range(CHUNKS):
        dk[...] = jnp.zeros_like(dk)
        dv[...] = jnp.zeros_like(dv)
        middle = [] if c == 0 else [(c - 1, 0)] if c < 3 else [(2, 0), (0, 1)]
        staged(lambda h: slope(h, c * CK, CK, 0), lambda h, dp: back(h, dp[...], c * CK, CK, 0, c + 1, 0), (p0, p1), middle)
        own[c][0:BLOCKS, 0:16, :] = (dk[...] * SCALE).astype(bf16).reshape(BLOCKS, 16, D)
        own[c][0:BLOCKS, 16:, :] = dv[...].astype(bf16).reshape(BLOCKS, 16, D)
        scatter.swap(c)
    dk[...] = jnp.zeros_like(dk)
    dv[...] = jnp.zeros_like(dv)

    def last(h):
        back(h, slope(h, PK, HALF, 0), PK, HALF, 0, 0, 0)
        back(h, slope(h, PK + HALF, HALF, HALF), PK + HALF, HALF, HALF, 0, HALF)

    def rows_out(h):
        dq_ref[:HALF, cols(h)] = (mm(kt[:, :PK + HALF], e_all[h, :PK + HALF, :HALF]) * SCALE).astype(bf16).T
        dq_ref[HALF:, cols(h)] = (mm(kt[...], e_all[h, :, HALF:]) * SCALE).astype(bf16).T
        o_ref[:, cols(h)] = ot[h].astype(bf16).T

    def send_home(src, dst, i):
        c = pltpu.make_async_copy(src, dst, local.at[i])
        c.start()
        return c

    heads_loop(0, 2, last, 2)
    scatter.stage(3, 0)
    scatter.stage(1, 1)
    scatter.stage(0, 2)
    heads_loop(2, 4, last, 2)
    heads_loop(4, HEADS, last)
    scatter.stage(2, 1)
    scatter.stage(1, 2)
    scatter.stage(0, 3)
    drkv_ref[:, 0:D] = (dk[...] * SCALE).astype(bf16)
    drkv_ref[:, D:] = dv[...].astype(bf16)
    home = [send_home(drkv_ref, drkv_hbm, 2)]
    heads_loop(0, 4, rows_out)
    half = HEADS * D // 2
    home.append(send_home(o_ref.at[:, :half], o_hbm.at[:, :half], 3))
    home.append(send_home(dq_ref.at[:, :half], dq_hbm.at[:, :half], 4))
    scatter.stage(3, 1)
    heads_loop(4, HEADS, rows_out)
    home.append(send_home(o_ref.at[:, half:], o_hbm.at[:, half:], 5))
    home.append(send_home(dq_ref.at[:, half:], dq_hbm.at[:, half:], 6))
    scatter.stage(2, 2)
    scatter.stage(1, 3)
    scatter.stage(3, 2)
    scatter.stage(2, 3)
    scatter.stage(3, 3)
    for c in home:
        c.wait()
    go.drain()


def on_device(queries, resp_kv, prefix_kv, grad_out, held_block, resp_prompt, resp_len):
    bufs = []
    for n in range(8):
        for i in range(3):
            bufs.append(pltpu.VMEM((3,) + (SIDE,) * (2 - i) + (16, D), bf16))
    sm = pl.BlockSpec(memory_space=pltpu.SMEM)
    vm = pl.BlockSpec(memory_space=pltpu.VMEM)
    hbm = pl.BlockSpec(memory_space=pl.ANY)
    sems = 18 + 8 * 7 + 8 * 9 + 4
    outs = pl.pallas_call(
        kernel,
        out_shape=(jax.ShapeDtypeStruct(queries.shape, bf16), jax.ShapeDtypeStruct(queries.shape, bf16),
                   jax.ShapeDtypeStruct(resp_kv.shape, bf16), jax.ShapeDtypeStruct((64, 256), f32)),
        in_specs=[vm] + [sm] * 3 + [hbm] * 2 + [vm] * 2,
        out_specs=(hbm,) * 3 + (vm,),
        scratch_shapes=[pltpu.VMEM((2, SIDE, SIDE, SIDE, 16, D), bf16)] * 8
        + [pltpu.VMEM((k, SIDE, SIDE, 16, D), bf16) for k in (3, 3, 2)]
        + [pltpu.VMEM((BLOCKS + 1, 32, D), bf16)] * 8 + [pltpu.VMEM((SIDE, SIDE, SIDE, 16, D), bf16)] * 8 + bufs
        + [pltpu.VMEM((ROWS, HEADS * D), bf16), pltpu.VMEM((ROWS, HEADS * D), bf16),
           pltpu.VMEM((NK, 2 * D), bf16), pltpu.VMEM((NK, 2 * D), bf16), pltpu.VMEM((D, NK), bf16),
           pltpu.VMEM((D, NK), bf16), pltpu.VMEM((HEADS, 2 * D, ROWS), bf16), pltpu.VMEM((HEADS, 2 * D, ROWS), bf16),
           pltpu.VMEM((HEADS, ROWS, D), bf16), pltpu.VMEM((HEADS, NK, ROWS), bf16),
           pltpu.SMEM((BLOCKS,), jnp.int32),
           pltpu.VMEM((CHUNKS + 1, HEADS, 1, ROWS), f32), pltpu.VMEM((HEADS, 1, ROWS), f32),
           pltpu.VMEM((HEADS, D, ROWS), f32), pltpu.VMEM((ROWS, HEADS * D), bf16), pltpu.VMEM((ROWS, HEADS * D), bf16),
           pltpu.VMEM((ROWS, 2 * D), bf16),
           pltpu.VMEM((ROWS, D), f32), pltpu.VMEM((ROWS, D), f32),
           pltpu.VMEM((CK, ROWS), f32), pltpu.VMEM((CK, ROWS), f32), pltpu.VMEM((CK, ROWS), bf16), pltpu.VMEM((CK, ROWS), bf16),
           pltpu.SemaphoreType.DMA((sems,)), pltpu.SemaphoreType.DMA((sems,)), pltpu.SemaphoreType.DMA((7,))],
        compiler_params=pltpu.CompilerParams(collective_id=0, has_side_effects=True, vmem_limit_bytes=62 * 2**20),
        name="shared",
    )(held_block, held_block, resp_prompt, resp_len, queries, grad_out, resp_kv, prefix_kv)
    return deliver(outs)


def deliver_kernel(*refs):
    n = len(refs) // 3
    sems = refs[-1]
    moves = []
    for i in range(n):
        src, dst, held = refs[i], refs[n + i], refs[2 * n + i]
        pieces = 4 if i < 2 else 1
        size = src.shape[0] // pieces
        for p in range(pieces):
            rows, k = slice(p * size, p * size + size), len(moves)
            moves.append((pltpu.make_async_copy(src.at[rows], held.at[rows], sems.at[0, k]),
                          pltpu.make_async_copy(held.at[rows], dst.at[rows], sems.at[1, k])))
    for bring, _ in moves:
        bring.start()
    for bring, leave in moves:
        bring.wait()
        leave.start()
    for _, leave in moves:
        leave.wait()


def deliver(arrays):
    hbm = pl.BlockSpec(memory_space=pl.ANY)
    return pl.pallas_call(
        deliver_kernel,
        out_shape=tuple(jax.ShapeDtypeStruct(a.shape, a.dtype) for a in arrays),
        in_specs=[hbm] * len(arrays),
        out_specs=(hbm,) * len(arrays),
        scratch_shapes=[pltpu.VMEM(a.shape, a.dtype) for a in arrays] + [pltpu.SemaphoreType.DMA((2, 10))],
        compiler_params=pltpu.CompilerParams(vmem_limit_bytes=62 * 2**20),
        name="deliver",
    )(*arrays)


def solution(mesh):
    rows = P("dp", None)
    return jax.shard_map(on_device, mesh=mesh, in_specs=(rows, rows, rows, rows, P(), P(), P()),
                         out_specs=(rows, rows, rows, rows), check_vma=False)
```

```python
import math

import jax
import jax.numpy as jnp
from jax import lax
from jax.experimental import pallas as pl
from jax.experimental.pallas import tpu as pltpu
from jax.sharding import PartitionSpec as P

f32, bf16 = jnp.float32, jnp.bfloat16
MESH = pl.DeviceIdType.MESH
NN = (((1,), (0,)), ((), ()))
SIDE = 4
D = 128
HEADS = 8
ROWS = 512
BLOCKS = 32
CHUNKS = 4
CK = 512
PK = CHUNKS * CK
NK = PK + ROWS
HALF = ROWS // 2
UNROLL = 4
SCALE = 1.0 / math.sqrt(D)
LOG2 = SCALE * math.log2(math.e)
ORDERS = ((0, 1, 2), (1, 2, 0), (2, 0, 1))
HOPS = (2, 1, 3)
PARTS = [(c, t) for c in range(CHUNKS) for t in range(2)]


def mm(a, b):
    return lax.dot_general(a, b, NN, preferred_element_type=f32)


def place():
    me = lax.axis_index("dp")
    return (me // 32, me // 8 % SIDE, me // 2 % SIDE), me % 2


def device(at, core):
    return ((at[0] * SIDE + at[1]) * SIDE + at[2]) * 2 + core


def moved(at, axis, step):
    return tuple((c + step) % SIDE if a == axis else c for a, c in enumerate(at))


class Sender:
    def __init__(self, send, recv):
        self.send, self.recv, self.count, self.all = send, recv, 0, []

    def __call__(self, src, dst, to):
        c = self.ready(src, dst, to)
        c.start()
        return c

    def ready(self, src, dst, to):
        i = self.count
        self.count += 1
        c = pltpu.make_async_remote_copy(src_ref=src, dst_ref=dst, send_sem=self.send.at[i], recv_sem=self.recv.at[i],
                                         device_id=(to,), device_id_type=MESH)
        self.all.append(c)
        return c

    def drain(self):
        for c in self.all:
            c.wait_send()


class Gather:
    def __init__(self, go, at, core, refs, stages):
        self.go, self.at, self.core, self.refs, self.stages = go, at, core, refs, stages
        self.flying = {}

    def put(self, x_ref):
        for n, (c, t) in enumerate(PARTS):
            a, b, _ = ORDERS[n % 3]
            self.stages[n % 3][n // 3, self.at[b], self.at[a]] = x_ref[16 * c:16 * c + 16, D * t:D * t + D]

    def start(self, k, i):
        a, b, _ = ORDERS[k]
        v = self.stages[k].at[:, self.at[b], self.at[a]] if i == 0 else self.stages[k].at[:, self.at[b]]
        self.flying[k, i] = [self.go(v, v, device(moved(self.at, ORDERS[k][i], s), self.core)) for s in HOPS]

    def start_last(self, n):
        a = ORDERS[n % 3][2]
        src, dst = self.stages[n % 3].at[n // 3], self.refs[n].at[self.core, self.at[a]]
        self.flying["part", n] = [self.go(src, dst, device(moved(self.at, a, s), self.core)) for s in HOPS]
        self.refs[n][self.core, self.at[a]] = self.stages[n % 3][n // 3]

    def wait(self, *key):
        for c in self.flying[key]:
            c.wait_recv()

    def ready_core(self, n):
        p, to = self.at[ORDERS[n % 3][2]], device(self.at, 1 - self.core)
        self.flying["core", n] = []
        for near in (None, 1, 2, 0):
            v = self.refs[n].at[self.core, p if near is None else (p + SIDE - HOPS[near]) % SIDE]
            self.flying["core", n].append(self.go.ready(v, v, to))

    def pass_on(self, n):
        for near, c in zip((None, 1, 2, 0), self.flying["core", n]):
            if near is not None:
                self.flying["part", n][near].wait_recv()
            c.start()


class Scatter:
    def __init__(self, go, at, core, held, prompt, own, peer, w, bufs, out):
        self.go, self.at, self.core, self.held, self.prompt = go, at, core, held, prompt
        self.own, self.peer, self.w, self.bufs, self.out = own, peer, w, bufs, out
        self.flying = {}
        self.coord = [[(at[a] + s) % SIDE for s in HOPS] for a in range(3)]
        self.dev = [[device(moved(at, a, s), core) for s in HOPS] for a in range(3)]
        self.other_core = device(at, 1 - core)

    def swap(self, c):
        self.flying[c] = self.go(self.own[c].at[0:BLOCKS], self.peer[c].at[0:BLOCKS], self.other_core)

    def fill(self, c):
        self.flying[c].wait_recv()
        mine = self.prompt[device(self.at, self.core)]
        other = self.prompt[device(self.at, 1 - self.core)]
        own, peer = self.own[c], self.peer[c]

        def body(j, _):
            for u in range(8):
                b = self.held[(j * 8 + u) * 2 + self.core]
                p, k = lax.shift_right_logical(b, 5), lax.bitwise_and(b, 31)
                v = own[jnp.where(p == mine, k, BLOCKS)] + peer[jnp.where(p == other, k, BLOCKS)]
                to = (j // 2, j % 2 * 2 + u // 4, u % 4)
                for t in range(2):
                    n = 2 * c + t
                    self.w[n][tuple(to[a] for a in ORDERS[n % 3])] = v[16 * t:16 * t + 16]
            return 0

        lax.fori_loop(0, 8, body, 0)

    def spot(self, n, i, k):
        return tuple(self.at[a] for a in ORDERS[n % 3][:i]) + (k,)

    def ready(self, c, i):
        for n in (2 * c, 2 * c + 1):
            a = ORDERS[n % 3][i]
            self.flying[n, i] = [
                self.go.ready(self.w[n].at[self.spot(n, i, self.coord[a][j])], self.bufs[3 * n + i].at[j], self.dev[a][j])
                for j in range(3)]

    def start(self, c, i):
        if (2 * c, i) not in self.flying:
            self.ready(c, i)
        for n in (2 * c, 2 * c + 1):
            for f in self.flying[n, i]:
                f.start()

    def add(self, c, i):
        for n in (2 * c, 2 * c + 1):
            for f in self.flying[n, i]:
                f.wait_recv()
            buf = self.bufs[3 * n + i]
            here = self.spot(n, i, self.at[ORDERS[n % 3][i]])
            total = (self.w[n][here].astype(f32) + buf[0].astype(f32)) + (buf[1].astype(f32) + buf[2].astype(f32))
            if i < 2:
                self.w[n][here] = total.astype(bf16)
            else:
                t = n % 2
                self.out[16 * c:16 * c + 16, D * t:D * t + D] = total

    def stage(self, c, s):
        if s == 0:
            self.fill(c)
            self.start(c, 0)
        else:
            self.add(c, s - 1)
            if s < 3:
                self.start(c, s)


def kernel(held_vec, held_ref, prompt_ref, len_ref, q_hbm, g_hbm, rkv_ref, x_ref, o_hbm, dq_hbm, drkv_hbm, out_ref, *rest):
    gref, stages, rest = rest[:8], rest[8:11], rest[11:]
    own, peer, w, bufs, rest = rest[:4], rest[4:8], rest[8:16], rest[16:40], rest[40:]
    q_ref, g_ref, kk, vv, kt, vt, q2t, g2t, gp, e_all, loc_ref, ms, ls, ot, o_ref, dq_ref, drkv_ref, dk, dv, s0, s1, p0, p1, send, recv, local = rest
    at, core = place()
    me = device(at, core)
    barrier = pltpu.get_barrier_semaphore()
    near = [device(moved(at, a, s), core) for a in range(3) for s in HOPS] + [device(at, 1 - core)]
    for n in near:
        pl.semaphore_signal(barrier, inc=1, device_id=(n,), device_id_type=MESH)
    q_in = pltpu.make_async_copy(q_hbm, q_ref, local.at[0])
    g_in = pltpu.make_async_copy(g_hbm, g_ref, local.at[1])
    q_in.start()
    g_in.start()
    go = Sender(send, recv)
    gather = Gather(go, at, core, gref, stages)
    gather.put(x_ref)
    pl.semaphore_wait(barrier, len(near))
    for k in range(3):
        gather.start(k, 0)

    for ref in (*own, *peer):
        ref[BLOCKS] = jnp.zeros((32, D), bf16)
    length = len_ref[me]
    live = lax.broadcasted_iota(jnp.int32, (1, ROWS), 1) < length
    tri = lax.broadcasted_iota(jnp.int32, (HALF, HALF), 0) <= lax.broadcasted_iota(jnp.int32, (HALF, HALF), 1)
    vv[:, D:] = jnp.ones((NK, D), bf16)

    def heads_loop(lo, hi, item, step=UNROLL):
        def body(i, _):
            for u in range(step):
                item(i * step + u)
            return 0
        lax.fori_loop(lo // step, hi // step, body, 0)

    def staged(ahead, item, slots, middle=None):
        slots[0][...] = ahead(0)

        def body(i, _):
            if middle is not None:
                pl.when(i == 1)(middle)
            for u in range(UNROLL):
                h = i * UNROLL + u
                slots[(u + 1) % 2][...] = ahead(lax.rem(h + 1, HEADS))
                item(h, slots[u % 2])
            return 0
        lax.fori_loop(0, HEADS // UNROLL, body, 0)

    def straight(ahead, item, slots, middle):
        slots[0][...] = ahead(0)
        for h in range(HEADS):
            if h == HEADS // 2:
                for job in middle:
                    scatter.stage(*job)
            if h + 1 < HEADS:
                slots[(h + 1) % 2][...] = ahead(h + 1)
            item(h, slots[h % 2])

    def cols(h):
        if isinstance(h, int):
            return slice(h * D, h * D + D)
        return pl.ds(pl.multiple_of(h * D, D), D)

    def prepare(h):
        qs = q_ref[:, cols(h)].astype(f32) * LOG2
        hi = qs.astype(bf16)
        lo = (qs - hi.astype(f32)).astype(bf16)
        q2t[h, 0:D] = hi.T
        q2t[h, D:] = lo.T
        g2t[h, 0:D] = g_ref[:, cols(h)].T
        g2t[h, D + 16:] = jnp.zeros((D - 16, ROWS), bf16)

    def place_keys(k0, kn, keys, vals):
        kk[k0:k0 + kn, 0:D] = keys
        kk[k0:k0 + kn, D:] = keys
        vv[k0:k0 + kn, 0:D] = vals

    def turn(k0, kn):
        kt[:, k0:k0 + kn] = kk[k0:k0 + kn, 0:D].T
        vt[:, k0:k0 + kn] = vv[k0:k0 + kn, 0:D].T

    def first(h):
        sa = mm(kk[PK:PK + HALF, :], q2t[h])
        sa = jnp.concatenate([jnp.where(tri, sa[:, :HALF], -1e30), sa[:, HALF:]], axis=1)
        sb = jnp.where(tri, mm(kk[PK + HALF:, :], q2t[h, :, HALF:]), -1e30)
        m = jnp.max(sa, axis=0, keepdims=True)
        m = jnp.concatenate([m[:, :HALF], jnp.maximum(m[:, HALF:], jnp.max(sb, axis=0, keepdims=True))], axis=1)
        ea = jnp.exp2(sa - m)
        eb = jnp.exp2(sb - m[:, HALF:])
        l = jnp.sum(ea, axis=0, keepdims=True)
        l = jnp.concatenate([l[:, :HALF], l[:, HALF:] + jnp.sum(eb, axis=0, keepdims=True)], axis=1)
        ea, eb = ea.astype(bf16), eb.astype(bf16)
        e_all[h, PK:PK + HALF, :] = ea
        e_all[h, PK + HALF:, HALF:] = eb
        oa = mm(vt[:, PK:PK + HALF], ea)
        ob = mm(vt[:, PK + HALF:], eb)
        ms[0, h] = m
        ls[h] = l
        ot[h, :, 0:HALF] = oa[:, :HALF]
        ot[h, :, HALF:] = oa[:, HALF:] + ob

    def forward(c, middle):
        k0 = c * CK

        def ahead(h):
            return mm(kk[k0:k0 + CK, :], q2t[h])

        def item(h, s):
            old = ms[c, h]
            m = jnp.maximum(old, jnp.max(s[...], axis=0, keepdims=True))
            e = jnp.exp2(s[...] - m)
            fade = jnp.exp2(old - m)
            ls[h] = ls[h] * fade + jnp.sum(e, axis=0, keepdims=True)
            e = e.astype(bf16)
            e_all[h, k0:k0 + CK, :] = e
            ot[h] = ot[h] * fade + mm(vt[:, k0:k0 + CK], e)
            ms[c + 1, h] = m
        staged(ahead, item, (s0, s1), middle)

    def finish(h):
        f = jnp.where(live, 1.0 / ls[h], 0.0)
        o = ot[h] * f
        ot[h] = o
        gt = g2t[h, 0:D].astype(f32)
        gt = jnp.where(live, gt, 0.0) * f
        neg = -jnp.sum(gt * o, axis=0, keepdims=True)
        gb = gt.astype(bf16)
        gp[h] = gb.T
        hi = neg.astype(bf16).astype(f32)
        sub = lax.broadcasted_iota(jnp.int32, (16, ROWS), 0)
        extra = jnp.where(sub == 0, hi, jnp.where(sub == 1, neg - hi, 0.0)).astype(bf16)
        g2t[h, 0:D] = gb
        g2t[h, D:D + 16] = extra

    def slope(h, k0, kn, r0):
        return mm(vv[k0:k0 + kn, :], g2t[h, :, r0:]).astype(bf16)

    def back(h, dp, k0, kn, r0, stage, a0):
        fade = jnp.exp2(ms[stage, h] - ms[CHUNKS, h]).astype(bf16)[:, r0:]
        e = e_all[h, k0:k0 + kn, r0:] * fade
        ds = e * dp
        e_all[h, k0:k0 + kn, r0:] = ds
        dk[a0:a0 + kn, :] += mm(ds, q_ref[r0:, cols(h)])
        dv[a0:a0 + kn, :] += mm(e, gp[h, r0:, :])

    def load_chunk(c):
        for n in (2 * c, 2 * c + 1):
            gather.wait("core", n)
        for b in range(BLOCKS):
            n = loc_ref[b]
            held_at = (lax.shift_right_logical(n, 5), lax.bitwise_and(lax.shift_right_logical(n, 3), 3),
                       lax.bitwise_and(lax.shift_right_logical(n, 1), 3))
            keys, vals = [gref[p][(lax.bitwise_and(n, 1),) + tuple(held_at[ORDERS[p % 3][i]] for i in (2, 1, 0))]
                          for p in (2 * c, 2 * c + 1)]
            place_keys(c * CK + 16 * b, 16, keys, vals)
        turn(c * CK, CK)

    place_keys(PK, ROWS, rkv_ref[:, 0:D], rkv_ref[:, D:])
    turn(PK, ROWS)
    q_in.wait()
    g_in.wait()
    heads_loop(0, HEADS, prepare)
    for k in range(3):
        gather.wait(k, 0)
        gather.start(k, 1)
    heads_loop(0, 4, first)
    for k in range(3):
        gather.wait(k, 1)
    for n in range(8):
        gather.start_last(n)
    heads_loop(4, HEADS, first)

    lane = lax.broadcasted_iota(jnp.int32, (1, 128), 1)
    held_row = held_vec[...].reshape(1, 128)
    base = prompt_ref[me] * BLOCKS
    for b in range(BLOCKS):
        loc_ref[b] = jnp.max(jnp.where(held_row == base + b, lane, 0))

    def pass_on(c):
        for n in (2 * c, 2 * c + 1):
            gather.pass_on(n)

    for n in range(8):
        gather.ready_core(n)
    pass_on(0)
    for c in range(CHUNKS):
        load_chunk(c)
        forward(c, (lambda: pass_on(c + 1)) if c + 1 < CHUNKS else None)
    heads_loop(0, HEADS, finish)

    scatter = Scatter(go, at, core, held_ref, prompt_ref, own, peer, w, bufs, out_ref)
    for c in range(CHUNKS):
        dk[...] = jnp.zeros_like(dk)
        dv[...] = jnp.zeros_like(dv)
        middle = [] if c == 0 else [(c - 1, 0)] if c < 3 else [(2, 0), (0, 1)]
        straight(lambda h: slope(h, c * CK, CK, 0), lambda h, dp: back(h, dp[...], c * CK, CK, 0, c + 1, 0), (p0, p1), middle)
        own[c][0:BLOCKS, 0:16, :] = (dk[...] * SCALE).astype(bf16).reshape(BLOCKS, 16, D)
        own[c][0:BLOCKS, 16:, :] = dv[...].astype(bf16).reshape(BLOCKS, 16, D)
        scatter.swap(c)
    dk[...] = jnp.zeros_like(dk)
    dv[...] = jnp.zeros_like(dv)

    def last(h):
        back(h, slope(h, PK, HALF, 0), PK, HALF, 0, 0, 0)
        back(h, slope(h, PK + HALF, HALF, HALF), PK + HALF, HALF, HALF, 0, HALF)

    def rows_out(h):
        dq_ref[:HALF, cols(h)] = (mm(kt[:, :PK + HALF], e_all[h, :PK + HALF, :HALF]) * SCALE).astype(bf16).T
        dq_ref[HALF:, cols(h)] = (mm(kt[...], e_all[h, :, HALF:]) * SCALE).astype(bf16).T
        o_ref[:, cols(h)] = ot[h].astype(bf16).T

    def send_home(src, dst, i):
        c = pltpu.make_async_copy(src, dst, local.at[i])
        c.start()
        return c

    heads_loop(0, 2, last, 2)
    scatter.stage(3, 0)
    scatter.stage(1, 1)
    scatter.stage(0, 2)
    heads_loop(2, 4, last, 2)
    heads_loop(4, HEADS, last)
    scatter.stage(2, 1)
    scatter.stage(1, 2)
    scatter.stage(0, 3)
    drkv_ref[:, 0:D] = (dk[...] * SCALE).astype(bf16)
    drkv_ref[:, D:] = dv[...].astype(bf16)
    home = [send_home(drkv_ref, drkv_hbm, 2)]
    heads_loop(0, 4, rows_out)
    half = HEADS * D // 2
    home.append(send_home(o_ref.at[:, :half], o_hbm.at[:, :half], 3))
    home.append(send_home(dq_ref.at[:, :half], dq_hbm.at[:, :half], 4))
    scatter.stage(3, 1)
    scatter.stage(2, 2)
    scatter.stage(1, 3)
    heads_loop(4, HEADS, rows_out)
    home.append(send_home(o_ref.at[:, half:], o_hbm.at[:, half:], 5))
    home.append(send_home(dq_ref.at[:, half:], dq_hbm.at[:, half:], 6))
    scatter.stage(2, 3)
    scatter.stage(3, 2)
    scatter.stage(3, 3)
    for c in home:
        c.wait()
    go.drain()


def on_device(queries, resp_kv, prefix_kv, grad_out, held_block, resp_prompt, resp_len):
    bufs = []
    for n in range(8):
        for i in range(3):
            bufs.append(pltpu.VMEM((3,) + (SIDE,) * (2 - i) + (16, D), bf16))
    sm = pl.BlockSpec(memory_space=pltpu.SMEM)
    vm = pl.BlockSpec(memory_space=pltpu.VMEM)
    hbm = pl.BlockSpec(memory_space=pl.ANY)
    sems = 18 + 8 * 7 + 8 * 9 + 4
    outs = pl.pallas_call(
        kernel,
        out_shape=(jax.ShapeDtypeStruct(queries.shape, bf16), jax.ShapeDtypeStruct(queries.shape, bf16),
                   jax.ShapeDtypeStruct(resp_kv.shape, bf16), jax.ShapeDtypeStruct((64, 256), f32)),
        in_specs=[vm] + [sm] * 3 + [hbm] * 2 + [vm] * 2,
        out_specs=(hbm,) * 3 + (vm,),
        scratch_shapes=[pltpu.VMEM((2, SIDE, SIDE, SIDE, 16, D), bf16)] * 8
        + [pltpu.VMEM((k, SIDE, SIDE, 16, D), bf16) for k in (3, 3, 2)]
        + [pltpu.VMEM((BLOCKS + 1, 32, D), bf16)] * 8 + [pltpu.VMEM((SIDE, SIDE, SIDE, 16, D), bf16)] * 8 + bufs
        + [pltpu.VMEM((ROWS, HEADS * D), bf16), pltpu.VMEM((ROWS, HEADS * D), bf16),
           pltpu.VMEM((NK, 2 * D), bf16), pltpu.VMEM((NK, 2 * D), bf16), pltpu.VMEM((D, NK), bf16),
           pltpu.VMEM((D, NK), bf16), pltpu.VMEM((HEADS, 2 * D, ROWS), bf16), pltpu.VMEM((HEADS, 2 * D, ROWS), bf16),
           pltpu.VMEM((HEADS, ROWS, D), bf16), pltpu.VMEM((HEADS, NK, ROWS), bf16),
           pltpu.SMEM((BLOCKS,), jnp.int32),
           pltpu.VMEM((CHUNKS + 1, HEADS, 1, ROWS), f32), pltpu.VMEM((HEADS, 1, ROWS), f32),
           pltpu.VMEM((HEADS, D, ROWS), f32), pltpu.VMEM((ROWS, HEADS * D), bf16), pltpu.VMEM((ROWS, HEADS * D), bf16),
           pltpu.VMEM((ROWS, 2 * D), bf16),
           pltpu.VMEM((ROWS, D), f32), pltpu.VMEM((ROWS, D), f32),
           pltpu.VMEM((CK, ROWS), f32), pltpu.VMEM((CK, ROWS), f32), pltpu.VMEM((CK, ROWS), bf16), pltpu.VMEM((CK, ROWS), bf16),
           pltpu.SemaphoreType.DMA((sems,)), pltpu.SemaphoreType.DMA((sems,)), pltpu.SemaphoreType.DMA((7,))],
        compiler_params=pltpu.CompilerParams(collective_id=0, has_side_effects=True, vmem_limit_bytes=62 * 2**20),
        name="shared",
    )(held_block, held_block, resp_prompt, resp_len, queries, grad_out, resp_kv, prefix_kv)
    return deliver(outs)


def deliver_kernel(*refs):
    n = len(refs) // 3
    sems = refs[-1]
    moves = []
    for i in range(n):
        src, dst, held = refs[i], refs[n + i], refs[2 * n + i]
        pieces = 4 if i < 2 else 1
        size = src.shape[0] // pieces
        for p in range(pieces):
            rows, k = slice(p * size, p * size + size), len(moves)
            moves.append((pltpu.make_async_copy(src.at[rows], held.at[rows], sems.at[0, k]),
                          pltpu.make_async_copy(held.at[rows], dst.at[rows], sems.at[1, k])))
    for bring, _ in moves:
        bring.start()
    for bring, leave in moves:
        bring.wait()
        leave.start()
    for _, leave in moves:
        leave.wait()


def deliver(arrays):
    hbm = pl.BlockSpec(memory_space=pl.ANY)
    return pl.pallas_call(
        deliver_kernel,
        out_shape=tuple(jax.ShapeDtypeStruct(a.shape, a.dtype) for a in arrays),
        in_specs=[hbm] * len(arrays),
        out_specs=(hbm,) * len(arrays),
        scratch_shapes=[pltpu.VMEM(a.shape, a.dtype) for a in arrays] + [pltpu.SemaphoreType.DMA((2, 10))],
        compiler_params=pltpu.CompilerParams(vmem_limit_bytes=62 * 2**20),
        name="deliver",
    )(*arrays)


def solution(mesh):
    rows = P("dp", None)
    return jax.shard_map(on_device, mesh=mesh, in_specs=(rows, rows, rows, rows, P(), P(), P()),
                         out_specs=(rows, rows, rows, rows), check_vma=False)
```
